128 devices in a mesh: img: 8 (over y, core), ori: 16 (over x, z).
Axes of the slice: x: 4, y: 4, z: 4, core: 2. Of those that a mesh axis runs over, the one named last changes fastest.
Arguments:
- images: bfloat16 [8192, 12288], P(('img', 'ori')), may hold values from -34 to 34
- projections: bfloat16 [9216, 12288], P('ori'), may hold values from -0.6 to 0.6
- search: int32 [512, 4], P(('img', 'ori')), may hold values from 0 to 15, all different within a row; in each aligned block of 4 rows (0 to 3, 4 to 7, ...) at most 2 rows name the same one
Outputs:
- weighted: bfloat16 [9216, 12288], P('ori', 'img')
- loglik: float32 [8192], P(('img', 'ori'))
The draws below stay inside these ranges and needn't reach their ends.
Inputs may be any that keep to these rules, and one draw needn't show every extreme that they name: `search`: each row names 4 different orientation blocks. In the 4 rows of one device no block is named by more than 2 rows, and some block is named by exactly 2 of them.
All inputs are finite; a program needn't handle non-finite values.
Results may differ from the reference program's by a relative error of at most 0.01.
Values may be sent and summed in bfloat16 or wider, within the bound.
A program may use at most 128 MiB of HBM per device.

```python
import math
import jax
import jax.numpy as jnp
import numpy as np
from jax import lax

TWOK = 12288
ORI_DEV = 576
GROUP = 16
GROUPS_DEV = 4
LISTED = 4
CAP = 2
GROUPS = 512
IMAGES = 8192
ORIS = 9216
N_ORI = 16


def shared_parts(key):
    scale_key = jax.random.fold_in(key, 0)
    col_scale = jnp.exp(jax.random.uniform(scale_key, (TWOK,), jnp.float32, math.log(0.3), math.log(3.0)))
    return col_scale


def draw_images(key, part):
    col_scale = shared_parts(key)
    key = jax.random.fold_in(key, 11)
    scale_key, noise_key = jax.random.split(key, 2)
    row_scale = jnp.exp(jax.random.uniform(scale_key, (IMAGES, 1), jnp.float32, math.log(0.25), math.log(2.5)))
    noise = jnp.clip(jax.random.normal(noise_key, (IMAGES, TWOK), jnp.float32), -4.0, 4.0)
    values = row_scale * noise / col_scale[None, :]
    return values.astype(jnp.bfloat16)


def draw_projections(key, part):
    col_scale = shared_parts(key)
    key = jax.random.fold_in(key, 23)
    scale_key, noise_key = jax.random.split(key)
    row_scale = jnp.exp(jax.random.uniform(scale_key, (ORIS, 1), jnp.float32, math.log(0.022), math.log(0.22)))
    row_scale = row_scale / math.sqrt(TWOK)
    noise = jnp.clip(jax.random.normal(noise_key, (ORIS, TWOK), jnp.float32), -4.0, 4.0)
    values = row_scale * col_scale[None, :] * noise
    return values.astype(jnp.bfloat16)


def routed_block(rng, own, number, rows, count, top, reach, skew):
    ranking = jax.random.permutation(rng, count)
    heavy_load, ordinary = shares(count, rows * top, reach, skew, True), shares(count, rows * top, reach, skew, False)
    places = jnp.arange(count)

    def named(tallies, rotation):
        used = int((tallies > 0).sum())
        fixed = max(1, used // 4)
        passed = fixed + (places - fixed + rotation * (used - fixed)) % max(1, count - fixed)
        return jnp.zeros((count,), jnp.int32).at[ranking[jnp.where(places < fixed, places, passed)]].set(jnp.asarray(tallies, jnp.int32))

    tallies = jnp.where(number % 4 == 0, named(heavy_load, number // 4), named(ordinary, number - number // 4 - 1))
    mixed = jax.random.permutation(jax.random.fold_in(own, 3), count)
    donor, taker = mixed[0:count // 2 * 2:2], mixed[1:count // 2 * 2:2]
    margin = jnp.minimum(tallies[donor] - 1, reach - tallies[taker]) // 2
    margin = jnp.where((donor == ranking[0]) | (taker == ranking[0]) | (tallies[taker] == 0), 0, jnp.maximum(margin, 0))
    passed = jax.random.randint(jax.random.fold_in(own, 4), (count // 2,), 0, 1 << 20) % (margin + 1)
    tallies = tallies.at[donor].add(-passed).at[taker].add(passed)
    labels = jnp.searchsorted(jnp.cumsum(tallies), jnp.arange(rows * top), side="right").astype(jnp.int32)
    grid = labels.reshape(top, rows).T
    grid = grid[jax.random.permutation(jax.random.fold_in(own, 1), rows)]
    rotation = jax.random.randint(jax.random.fold_in(own, 2), (rows, 1), 0, top)
    return jnp.take_along_axis(grid, (jnp.arange(top)[None, :] + rotation) % top, axis=1)


def shares(count, total, most, skew, full):
    loads = [(1 << 20) // math.isqrt(grade ** skew) + 1 for grade in range(1, count + 1)]
    largest = most if full else min(most, max(-(-total // count), total * loads[0] // sum(loads)))
    least = 1 if total - largest >= count - 1 else 0
    counts, rest = [largest] + [least] * (count - 1), total - largest - least * (count - 1)
    while rest > 0:
        free = [i for i in range(1, count) if counts[i] < largest] or [i for i in range(1, count) if counts[i] < most]
        mass, budget = sum([loads[i] for i in free]), rest
        for i in free:
            more = min(most - counts[i], max(1, budget * loads[i] // mass), rest)
            counts[i] = counts[i] + more
            rest = rest - more
    return np.array(counts)


def setup_inputs(seed: int = 0) -> dict:
    streams_of = jax.random.split(jax.random.key(seed), 4)
    images = draw_images(jax.random.fold_in(streams_of[3], 71), 0)
    projections = draw_projections(jax.random.fold_in(streams_of[3], 71), 0)
    search_keys = jax.random.split(jax.random.fold_in(streams_of[2], 1), GROUPS // GROUPS_DEV)
    search_turns = jax.random.permutation(jax.random.fold_in(streams_of[2], 3), GROUPS // GROUPS_DEV)
    search = jax.vmap(lambda own, number: routed_block(jax.random.fold_in(streams_of[2], 2), own, number, GROUPS_DEV, N_ORI, LISTED, CAP, 2))(search_keys, search_turns).reshape((GROUPS, LISTED))
    return {"images": images, "projections": projections, "search": search}


def reference(images, projections, search):
    columns = images.shape[1]
    blocks = projections.astype(jnp.float32).reshape(N_ORI, ORI_DEV, columns)
    half_norm = 0.5 * jnp.sum(blocks * blocks, axis=2)
    grouped = images.astype(jnp.float32).reshape(GROUPS, GROUP, columns)

    def group_step(running, inputs):
        group_images, block_ids = inputs
        chosen = blocks[block_ids]
        scores = jnp.einsum("ik,ljk->ilj", group_images, chosen) - half_norm[block_ids][None, :, :]
        highest = jnp.max(scores, axis=(1, 2))
        loglik = highest + jnp.log(jnp.sum(jnp.exp(scores - highest[:, None, None]), axis=(1, 2)))
        rounded = jnp.exp(scores - loglik[:, None, None]).astype(jnp.bfloat16)
        responsibility = lax.optimization_barrier(rounded).astype(jnp.float32)
        contrib = jnp.einsum("ilj,ik->ljk", responsibility, group_images)
        running = running.at[block_ids].add(contrib)
        return running, loglik

    start_sums = jnp.zeros((N_ORI, ORI_DEV, columns), jnp.float32)
    weighted, loglik = lax.scan(group_step, start_sums, (grouped, search))
    return weighted.reshape(ORIS, columns).astype(jnp.bfloat16), loglik.reshape(-1)
```

```python
import functools
import math

import jax
import jax.numpy as jnp
from jax import lax
from jax.experimental import pallas as pl
from jax.experimental.pallas import tpu as pltpu
from jax.sharding import PartitionSpec as P

MESH = pl.DeviceIdType.MESH
SIDE = 4
CORES = 2
SLOTS = 2
LANES = 128
NO_SCORE = -3.0e38


def ring(position, step):
    return lax.rem(position + step + SIDE, SIDE)


def coordinates():
    m, b = lax.axis_index("img"), lax.axis_index("ori")
    return lax.div(m, CORES), lax.rem(m, CORES), lax.div(b, SIDE), lax.rem(b, SIDE)


def at_img(y, c):
    return {"img": y * CORES + c, "ori": lax.axis_index("ori")}


def at_ori(x, z):
    return {"img": lax.axis_index("img"), "ori": x * SIDE + z}


def remote(source, target, send, recv, device):
    return pltpu.make_async_remote_copy(
        src_ref=source,
        dst_ref=target,
        send_sem=send,
        recv_sem=recv,
        device_id=device,
        device_id_type=MESH,
    )


def greet(devices):
    barrier = pltpu.get_barrier_semaphore()
    for device in devices:
        pl.semaphore_signal(barrier, inc=1, device_id=device, device_id_type=MESH)
    pl.semaphore_wait(barrier, len(devices))


TURNS = [(0, 0), (0, 1), (1, 0), (1, 1), (3, 0), (3, 1), (2, 0), (2, 1)]


def slot_table(search):
    blocks = SIDE * SIDE
    lane = lax.broadcasted_iota(jnp.int32, (8, LANES), 1)
    b, s = lax.rem(lane, blocks), lax.div(lane, blocks)
    table = jnp.full((8, LANES), -1.0, jnp.float32)
    rank = jnp.zeros((8, LANES), jnp.int32)
    for g in range(search.shape[0]):
        hit = b == search[g, 0]
        for n in range(1, search.shape[1]):
            hit = hit | (b == search[g, n])
        table = jnp.where(hit & (rank == s), float(g), table)
        rank = rank + hit.astype(jnp.int32)
    return table


def spread_kernel(
    search,
    images,
    xa,
    xb,
    tables,
    told,
    home_sem,
    turn_send,
    turn_recv,
    near_send,
    near_recv,
    far_send,
    far_recv,
    told_send,
    told_recv,
    table_send,
    table_recv,
):
    y, c, x, z = coordinates()
    rows, half = xa.shape[2], xa.shape[3]
    mid = rows // 2
    me = y * CORES + c
    img_peers = [at_img(ring(y, dy), lax.rem(c + dc, CORES)) for dy, dc in TURNS[1:]]
    steps = [(dx, dz) for dx in range(SIDE) for dz in range(SIDE) if (dx, dz) != (0, 0)]
    plane = [at_ori(ring(x, dx), ring(z, dz)) for dx, dz in steps]
    ori_peers = [at_ori(ring(x, 1), z), at_ori(ring(x, -1), z), at_ori(x, ring(z, 1)), at_ori(x, ring(z, -1))]
    greet(img_peers + plane)

    def columns(m, part):
        return images.at[:, pl.ds(pl.multiple_of(m * (2 * half) + part * half, 128), half)]

    turned, home = [], []
    for k, (dy, dc) in enumerate(TURNS):
        to_y, to_c = ring(y, dy), lax.rem(c + dc, CORES)
        to_m = to_y * CORES + to_c
        for part, (line, place) in enumerate(((xa, x), (xb, z))):
            if k == 0:
                copy = pltpu.make_async_copy(columns(to_m, part), line.at[place, me], home_sem.at[part])
                home.append(copy)
            else:
                copy = remote(
                    columns(to_m, part), line.at[place, me], turn_send.at[k, part], turn_recv.at[k, part], at_img(to_y, to_c)
                )
                turned.append(copy)
            copy.start()
    told[me] = slot_table(search)
    tells = [
        remote(told.at[me], told.at[me], told_send.at[k], told_recv.at[k], peer) for k, peer in enumerate(img_peers)
    ]
    for copy in tells:
        copy.start()

    near = {}
    far = []

    def start_near(k):
        dy, dc = TURNS[k]
        source = ring(y, -dy) * CORES + lax.rem(c + dc, CORES)
        for way in range(4):
            line, place = (xa, x) if way < 2 else (xb, z)
            block = line.at[place, source]
            near[k, way] = remote(block, block, near_send.at[k, way], near_recv.at[k, way], ori_peers[way])
            near[k, way].start()

    def start_far(k):
        dy, dc = TURNS[k]
        source = ring(y, -dy) * CORES + lax.rem(c + dc, CORES)
        for way in range(4):
            line, place = (xa, x) if way < 2 else (xb, z)
            forward = way % 2 == 0
            near[k, way].wait_recv()
            block = line.at[ring(place, -1 if forward else 1), source, pl.ds(0 if forward else mid, mid)]
            copy = remote(block, block, far_send.at[k, way], far_recv.at[k, way], ori_peers[way])
            copy.start()
            far.append(copy)

    for k in range(len(TURNS)):
        for part in range(2):
            if k == 0:
                home[part].wait()
            else:
                turned[2 * (k - 1) + part].wait_recv()
        start_near(k)
        if k > 0:
            start_far(k - 1)
    for copy in tells:
        copy.wait_recv()
    b = x * SIDE + z
    sublane = lax.broadcasted_iota(jnp.int32, (8, LANES), 0)
    gathered = told[0]
    for m in range(1, told.shape[0]):
        gathered = jnp.where(sublane == m, told[m], gathered)
    tables[b] = gathered
    spreads = [
        remote(tables.at[b], tables.at[b], table_send.at[k], table_recv.at[k], peer) for k, peer in enumerate(plane)
    ]
    for copy in spreads:
        copy.start()
    start_far(len(TURNS) - 1)
    for copy in tells:
        copy.wait_send()
    for copy in spreads:
        copy.wait()
    for copy in turned + list(near.values()):
        copy.wait_send()
    for copy in far:
        copy.wait()


def spread(search, images):
    rows, columns = images.shape
    blocks = SIDE * SIDE
    planes = SIDE * CORES
    half = columns // planes // 2
    line = jax.ShapeDtypeStruct((SIDE, planes, rows, half), images.dtype)
    turns = len(TURNS)
    return pl.pallas_call(
        spread_kernel,
        out_shape=(line, line, jax.ShapeDtypeStruct((blocks, planes, LANES), jnp.float32)),
        in_specs=[pl.BlockSpec(memory_space=pltpu.SMEM), pl.BlockSpec(memory_space=pl.ANY)],
        out_specs=(
            pl.BlockSpec(memory_space=pl.ANY),
            pl.BlockSpec(memory_space=pl.ANY),
            pl.BlockSpec(memory_space=pltpu.VMEM),
        ),
        scratch_shapes=[
            pltpu.VMEM((planes, 8, LANES), jnp.float32),
            pltpu.SemaphoreType.DMA((2,)),
            pltpu.SemaphoreType.DMA((turns, 2)),
            pltpu.SemaphoreType.DMA((turns, 2)),
            pltpu.SemaphoreType.DMA((turns, 4)),
            pltpu.SemaphoreType.DMA((turns, 4)),
            pltpu.SemaphoreType.DMA((turns, 4)),
            pltpu.SemaphoreType.DMA((turns, 4)),
            pltpu.SemaphoreType.DMA((planes - 1,)),
            pltpu.SemaphoreType.DMA((planes - 1,)),
            pltpu.SemaphoreType.DMA((blocks - 1,)),
            pltpu.SemaphoreType.DMA((blocks - 1,)),
        ],
        compiler_params=pltpu.CompilerParams(collective_id=0, has_side_effects=True),
        cost_estimate=pl.CostEstimate(flops=0, bytes_accessed=16 * 2**20, transcendentals=0),
    )(search, images)


ROUNDS = [2, 1, 3, 0]


def main_kernel(
    tables,
    xa_hbm,
    xb_hbm,
    projections,
    weighted,
    loglik,
    xa,
    xb,
    proj,
    picks,
    arrived,
    out_a,
    out_b,
    pair_out,
    pair_in,
    kept,
    y_in,
    stats,
    resp,
    total,
    load_sem,
    a_send,
    a_recv,
    b_send,
    b_recv,
    pair_send,
    pair_recv,
    y_send,
    y_recv,
    stat_send,
    stat_recv,
    r_send,
    r_recv,
    rc_send,
    rc_recv,
):
    y, c, x, z = coordinates()
    me = y * CORES + c
    block = x * SIDE + z
    blocks = SIDE * SIDE
    other = 1 - c
    group, half = arrived.shape[5], arrived.shape[6] // 2
    slice_columns = 2 * half
    oris = proj.shape[0]
    lanes = kept.shape[2]

    loads = [
        pltpu.make_async_copy(xa_hbm, xa, load_sem.at[0]),
        pltpu.make_async_copy(xb_hbm, xb, load_sem.at[1]),
        pltpu.make_async_copy(
            projections.at[:, pl.ds(pl.multiple_of(me * slice_columns, 128), slice_columns)], proj, load_sem.at[2]
        ),
    ]
    for copy in loads:
        copy.start()
    ori_peers = [
        (dx, dz, at_ori(ring(x, dx), ring(z, dz))) for dx in range(SIDE) for dz in range(SIDE) if (dx, dz) != (0, 0)
    ]
    partner = at_img(y, other)
    y_peers = [at_img(ring(y, d), c) for d in range(1, SIDE)]
    greet([device for _, _, device in ori_peers] + [partner] + y_peers)
    loads[0].wait()
    loads[1].wait()

    planes = xa.shape[1]
    lane_row = lax.broadcasted_iota(jnp.int32, (LANES, LANES), 0)
    for d in range(SIDE):
        for s in range(SLOTS):
            for part, dest in enumerate((x * SIDE + ring(z, d), ring(x, d) * SIDE + z)):
                column = jnp.where(lane_row == s * blocks + dest, 1.0, 0.0)
                for p in range(SIDE):
                    home = p * SIDE + z if part == 0 else x * SIDE + p
                    picks[part, d, s, p] = jnp.dot(tables[home], column, preferred_element_type=jnp.float32)

    def fill(j):
        home_y = ring(y, ROUNDS[j])
        slot = j % 2

        def step(n, carry):
            cc, p = lax.div(n, SIDE), lax.rem(n, SIDE)
            m = home_y * CORES + cc
            for part, line in enumerate((xa, xb)):
                choices = [line[p, m, g * group : (g + 1) * group, :] for g in range(line.shape[2] // group)]
                for d in range(SIDE):
                    for s in range(SLOTS):
                        pick = jnp.broadcast_to(picks[part, d, s, p, pl.ds(m, 1), :], (group, LANES))
                        pick = jnp.concatenate([pick.astype(jnp.bfloat16)] * (half // LANES), axis=1)
                        value = choices[0]
                        for g in range(1, len(choices)):
                            value = jnp.where(pick == g, choices[g], value)
                        if d and part == 0:
                            out_a[slot, d - 1, cc, s, p] = value
                        elif d:
                            out_b[slot, d - 1, cc, s, p] = value
                        elif part == 0:
                            arrived[j, cc, s, z, p, :, 0:half] = value
                        else:
                            arrived[j, cc, s, p, x, :, half : 2 * half] = value
            return carry

        lax.fori_loop(0, CORES * SIDE, step, 0)

    moves = {}

    def send(j):
        slot = j % 2
        moves[j] = []
        for d in (2, 1, 3):
            moves[j].append(
                remote(
                    out_a.at[slot, d - 1],
                    arrived.at[j, :, :, z, :, :, pl.ds(0, half)],
                    a_send.at[slot, d - 1],
                    a_recv.at[j, d - 1],
                    at_ori(x, ring(z, d)),
                )
            )
            moves[j].append(
                remote(
                    out_b.at[slot, d - 1],
                    arrived.at[j, :, :, :, x, :, pl.ds(half, half)],
                    b_send.at[slot, d - 1],
                    b_recv.at[j, d - 1],
                    at_ori(ring(x, d), z),
                )
            )
        for copy in moves[j]:
            copy.start()

    fill(0)
    send(0)
    fill(1)
    send(1)
    loads[2].wait()
    wide = proj[...].astype(jnp.float32)
    half_norm = 0.5 * jnp.sum(wide * wide, axis=1, keepdims=True)

    def scores(j, cc):
        rows = arrived[j, cc].reshape(lanes, slice_columns)
        return (
            lax.dot_general(proj[...], rows, (((1,), (1,)), ((), ())), preferred_element_type=jnp.float32) - half_norm
        )

    pairs, sums = [], []
    for j in range(SIDE):
        for copy in moves[j]:
            copy.wait_recv()
        if j + 2 < SIDE:
            for copy in moves[j]:
                copy.wait_send()
            fill(j + 2)
            send(j + 2)
        slot = j % 2
        if j >= 2:
            pairs[j - 2].wait_send()
        pair_out[slot] = scores(j, other)
        copy = remote(pair_out.at[slot], pair_in.at[j], pair_send.at[slot], pair_recv.at[j], partner)
        copy.start()
        pairs.append(copy)
        kept[j] = scores(j, c)
        copy.wait_recv()
        kept[j] += pair_in[j]
        d = ROUNDS[j]
        if d:
            copy = remote(kept.at[j], y_in.at[d - 1], y_send.at[d - 1], y_recv.at[d - 1], y_peers[d - 1])
            copy.start()
            sums.append(copy)
    for j in (2, 3):
        for copy in moves[j]:
            copy.wait_send()
        pairs[j].wait_send()
    for copy in sums:
        copy.wait()

    last = SIDE - 1
    kept[last] = kept[last] + y_in[0] + y_in[1] + y_in[2]
    highest = jnp.max(kept[last], axis=0, keepdims=True)
    weight = jnp.sum(jnp.exp(kept[last] - highest), axis=0, keepdims=True)
    which = lax.broadcasted_iota(jnp.int32, (8, lanes), 0)
    stats[block] = jnp.where(which == 0, highest, weight)
    told = []
    for dx, dz, device in ori_peers:
        k = dx * SIDE + dz
        told.append(remote(stats.at[block], stats.at[block], stat_send.at[k], stat_recv.at[k], device))
        told[-1].start()
    for copy in told:
        copy.wait()

    tops, masses = stats[:, 0, :], stats[:, 1, :]
    images = lanes // SLOTS
    home_row = lax.broadcasted_iota(jnp.int32, (blocks, images), 0)
    home_lane = lax.div(lax.broadcasted_iota(jnp.int32, (blocks, images), 1), group)
    spot = lax.rem(home_lane, SIDE) * SIDE + lax.div(home_lane, SIDE)
    widen = jnp.where(home_row == spot, 1.0, 0.0)
    plane = tables[:, pl.ds(me, 1), :].reshape(blocks, LANES)
    named = lax.dot_general(plane, widen, (((0,), (0,)), ((), ())), preferred_element_type=jnp.float32)
    named = jnp.concatenate([named[s * blocks : (s + 1) * blocks] for s in range(SLOTS)], axis=1)
    block_row = lax.broadcasted_iota(jnp.int32, (blocks, lanes), 0)
    own = jnp.sum(jnp.where(block_row == block, named, 0.0), axis=0, keepdims=True)
    norm = jnp.zeros((1, lanes), jnp.float32)
    for g in range(loglik.shape[0]):
        listed = named == g
        top = jnp.max(jnp.where(listed, tops, NO_SCORE), axis=0, keepdims=True)
        top = jnp.maximum(top[:, :images], top[:, images:])
        top2 = jnp.concatenate([top, top], axis=1)
        mass = jnp.where(listed, jnp.exp(jnp.minimum(tops - top2, 0.0)) * masses, 0.0)
        mass = jnp.sum(mass, axis=0, keepdims=True)
        value = top + jnp.log(mass[:, :images] + mass[:, images:])
        loglik[pl.ds(g, 1), :] = value
        norm = jnp.where(own == g, jnp.concatenate([value, value], axis=1), norm)
    resp[0, c] = jnp.where(own >= 0, jnp.exp(kept[last] - norm), 0.0).astype(jnp.bfloat16)

    sent, crossed = {}, {}
    for d in (2, 1, 3):
        sent[d] = remote(resp.at[0, c], resp.at[d, c], r_send.at[d], r_recv.at[d], at_img(ring(y, -d), c))
        sent[d].start()
    crossed[0] = remote(resp.at[0, c], resp.at[0, c], rc_send.at[0], rc_recv.at[0], partner)
    crossed[0].start()

    tile = 512

    def add(d, cc, first=False, final=False):
        j = ROUNDS.index(d)
        for t in range(slice_columns // tile):
            cols = slice(t * tile, (t + 1) * tile)
            rows = arrived[j, cc, :, :, :, :, cols].reshape(lanes, tile)
            part = jnp.dot(resp[d, cc], rows, preferred_element_type=jnp.float32)
            if not first:
                part = part + total[:, cols]
            if final:
                weighted[:, cols] = part.astype(weighted.dtype)
            else:
                total[:, cols] = part

    add(0, c, first=True)
    crossed[0].wait_recv()
    add(0, other)
    for d in (1, 3, 2):
        sent[d].wait_recv()
        crossed[d] = remote(resp.at[d, c], resp.at[d, c], rc_send.at[d], rc_recv.at[d], partner)
        crossed[d].start()
        add(d, c)
        crossed[d].wait_recv()
        add(d, other, final=d == 2)
    for d in range(SIDE):
        if d:
            sent[d].wait_send()
        crossed[d].wait_send()


def per_device(images, projections, search):
    blocks = SIDE * SIDE
    groups, _ = search.shape
    rows, columns = images.shape
    planes = SIDE * CORES
    group = rows // groups
    slice_columns = columns // planes
    half = slice_columns // 2
    oris = projections.shape[0]
    lanes = blocks * SLOTS * group
    images_plane = blocks * group

    xa, xb, tables = spread(search, images)
    vmem, anywhere = pl.BlockSpec(memory_space=pltpu.VMEM), pl.BlockSpec(memory_space=pl.ANY)
    bf16, f32, dma = jnp.bfloat16, jnp.float32, pltpu.SemaphoreType.DMA
    peers = SIDE - 1
    weighted, loglik = pl.pallas_call(
        main_kernel,
        out_shape=(
            jax.ShapeDtypeStruct((oris, slice_columns), bf16),
            jax.ShapeDtypeStruct((groups, images_plane), f32),
        ),
        in_specs=[vmem, anywhere, anywhere, anywhere],
        out_specs=(vmem, vmem),
        scratch_shapes=[
            pltpu.VMEM((SIDE, planes, rows, half), bf16),
            pltpu.VMEM((SIDE, planes, rows, half), bf16),
            pltpu.VMEM((oris, slice_columns), bf16),
            pltpu.VMEM((2, SIDE, SLOTS, SIDE, planes, LANES), f32),
            pltpu.VMEM((SIDE, CORES, SLOTS, SIDE, SIDE, group, slice_columns), bf16),
            pltpu.VMEM((2, peers, CORES, SLOTS, SIDE, group, half), bf16),
            pltpu.VMEM((2, peers, CORES, SLOTS, SIDE, group, half), bf16),
            pltpu.VMEM((2, oris, lanes), f32),
            pltpu.VMEM((SIDE, oris, lanes), f32),
            pltpu.VMEM((SIDE, oris, lanes), f32),
            pltpu.VMEM((peers, oris, lanes), f32),
            pltpu.VMEM((blocks, 8, lanes), f32),
            pltpu.VMEM((SIDE, CORES, oris, lanes), bf16),
            pltpu.VMEM((oris, slice_columns), f32),
            dma((3,)),
            dma((2, peers)),
            dma((SIDE, peers)),
            dma((2, peers)),
            dma((SIDE, peers)),
            dma((2,)),
            dma((SIDE,)),
            dma((peers,)),
            dma((peers,)),
            dma((blocks,)),
            dma((blocks,)),
            dma((SIDE,)),
            dma((SIDE,)),
            dma((SIDE,)),
            dma((SIDE,)),
        ],
        compiler_params=pltpu.CompilerParams(collective_id=1, has_side_effects=True, vmem_limit_bytes=62 * 2**20),
        cost_estimate=pl.CostEstimate(flops=15 * 10**9, bytes_accessed=32 * 2**20, transcendentals=10**6),
    )(tables, xa, xb, projections)
    b = lax.axis_index("ori")
    home = lax.rem(b, SIDE) * SIDE + lax.div(b, SIDE)
    loglik = lax.dynamic_index_in_dim(loglik.reshape(groups, blocks, group), home, 1, False)
    return weighted, loglik.reshape(-1)


def solution(mesh):
    placed = (P(("img", "ori"), None), P("ori", None), P(("img", "ori"), None))
    return jax.shard_map(
        per_device,
        mesh=mesh,
        in_specs=placed,
        out_specs=(P("ori", "img"), P(("img", "ori"))),
        check_vma=False,
    )
```

```python
import jax
import jax.numpy as jnp
from jax import lax
from jax.experimental import pallas as pl
from jax.experimental.pallas import tpu as pltpu
from jax.sharding import PartitionSpec as P

MESH = pl.DeviceIdType.MESH
SIDE = 4
CORES = 2
PLANES = SIDE * CORES
BLOCKS = SIDE * SIDE
SLOTS = 2
LANES = 128
BATCHES = 2
AHEAD = 3
NO_SCORE = -3.0e38

ROUNDS = [(2, 2), (1, 3), (3, 1), (0, 0)]


def ring(position, step):
    return lax.rem(position + step + SIDE, SIDE)


def at_img(y, c):
    return {"img": y * CORES + c, "ori": lax.axis_index("ori")}


def at_ori(x, z):
    return {"img": lax.axis_index("img"), "ori": x * SIDE + z}


def remote(source, target, send, recv, device):
    return pltpu.make_async_remote_copy(
        src_ref=source,
        dst_ref=target,
        send_sem=send,
        recv_sem=recv,
        device_id=device,
        device_id_type=MESH,
    )


def greet(devices):
    barrier = pltpu.get_barrier_semaphore()
    for device in devices:
        pl.semaphore_signal(barrier, inc=1, device_id=device, device_id_type=MESH)
    pl.semaphore_wait(barrier, len(devices))


def slot_table(search):
    lane = lax.broadcasted_iota(jnp.int32, (8, LANES), 1)
    b, s = lax.rem(lane, BLOCKS), lax.div(lane, BLOCKS)
    table = jnp.full((8, LANES), -1.0, jnp.float32)
    rank = jnp.zeros((8, LANES), jnp.int32)
    for g in range(search.shape[0]):
        hit = b == search[g, 0]
        for n in range(1, search.shape[1]):
            hit = hit | (b == search[g, n])
        table = jnp.where(hit & (rank == s), float(g), table)
        rank = rank + hit.astype(jnp.int32)
    return table


def kernel(
    search,
    images,
    projections,
    weighted,
    loglik,
    xa,
    xb,
    told,
    tables,
    picks,
    proj,
    arrived,
    out_a,
    out_b,
    pair_out,
    pair_in,
    kept,
    y_in,
    stats,
    resp,
    total,
    load_sem,
    turn_send,
    turn_recv,
    told_send,
    told_recv,
    table_send,
    table_recv,
    near_send,
    near_recv,
    far_send,
    far_recv,
    a_send,
    a_recv,
    b_send,
    b_recv,
    pair_send,
    pair_recv,
    y_send,
    y_recv,
    stat_send,
    stat_recv,
    r_send,
    r_recv,
    rc_send,
    rc_recv,
):
    me, block = lax.axis_index("img"), lax.axis_index("ori")
    y, c = lax.div(me, CORES), lax.rem(me, CORES)
    x, z = lax.div(block, SIDE), lax.rem(block, SIDE)
    other = 1 - c
    rows, half = xa.shape[2], xa.shape[3]
    mid = rows // 2
    group = arrived.shape[7]
    groups = rows // group
    slice_columns = 2 * half
    lanes = kept.shape[3]
    partner = at_img(y, other)
    steps = [(dx, dz) for dx in range(SIDE) for dz in range(SIDE) if (dx, dz) != (0, 0)]
    ori_peers = [at_ori(ring(x, dx), ring(z, dz)) for dx, dz in steps]
    img_peers = [partner] + [at_img(ring(y, d), cc) for d in range(1, SIDE) for cc in range(CORES)]
    neighbours = [at_ori(ring(x, 1), z), at_ori(ring(x, -1), z), at_ori(x, ring(z, 1)), at_ori(x, ring(z, -1))]


    def columns(m, part):
        return images.at[:, pl.ds(pl.multiple_of(m * slice_columns + part * half, LANES), half)]

    def line(part):
        return (xa, x) if part == 0 else (xb, z)

    home = []
    for part in range(2):
        ref, place = line(part)
        home.append(pltpu.make_async_copy(columns(me, part), ref.at[place, me], load_sem.at[part]))
    load = pltpu.make_async_copy(
        projections.at[:, pl.ds(pl.multiple_of(me * slice_columns, LANES), slice_columns)], proj, load_sem.at[2]
    )
    for copy in home + [load]:
        copy.start()
    told[me] = slot_table(search)
    greet(img_peers + ori_peers)
    receivers = [(0, other)] + [(d, cc) for d in (2, 1 + 2 * c, 3 - 2 * c) for cc in range(CORES)]
    tells, turns = [], {}
    for k, (d, cc) in enumerate(receivers):
        tells.append(remote(told.at[me], told.at[me], told_send.at[k], told_recv.at[d, c], at_img(ring(y, -d), cc)))
        tells[-1].start()
    for k, (d, cc) in enumerate(receivers):
        for part in range(2):
            ref, place = line(part)
            turns[k, part] = remote(
                columns(ring(y, -d) * CORES + cc, part),
                ref.at[place, me],
                turn_send.at[k, part],
                turn_recv.at[d, c, part],
                at_img(ring(y, -d), cc),
            )
            turns[k, part].start()

    sources = [(0, c), (0, other), (2, 0), (2, 1), (1, 0), (3, 1), (3, 0), (1, 1)]

    def source(k):
        d, cc = sources[k]
        return ring(y, d) * CORES + cc

    near, far = {}, {}

    def start_near(k):
        d, cc = sources[k]
        for part in range(2):
            ref, place = line(part)
            block_ref = ref.at[place, source(k)]
            if k == 0:
                home[part].wait()
            else:
                remote(
                    block_ref, block_ref, turn_send.at[k - 1, part], turn_recv.at[d, cc, part], partner
                ).wait_recv()
            for way in (2 * part, 2 * part + 1):
                near[k, way] = remote(
                    block_ref, block_ref, near_send.at[k, way], near_recv.at[k, way], neighbours[way]
                )
                near[k, way].start()

    def start_far(k):
        for way in range(4):
            ref, place = line(way // 2)
            forward = way % 2 == 0
            near[k, way].wait_recv()
            block_ref = ref.at[ring(place, -1 if forward else 1), source(k), pl.ds(0 if forward else mid, mid)]
            far[k, way] = remote(block_ref, block_ref, far_send.at[k, way], far_recv.at[k, way], neighbours[way])
            far[k, way].start()

    def wait_far(k):
        for way in range(4):
            far[k, way].wait_recv()

    start_near(0)
    for d in range(SIDE):
        for cc in range(CORES) if d else (other,):
            tile = told.at[ring(y, d) * CORES + cc]
            remote(tile, tile, told_send.at[0], told_recv.at[d, cc], partner).wait_recv()
    sublane = lax.broadcasted_iota(jnp.int32, (PLANES, LANES), 0)
    gathered = told[0]
    for m in range(1, PLANES):
        gathered = jnp.where(sublane == m, told[m], gathered)
    tables[block] = gathered
    spreads = [
        remote(tables.at[block], tables.at[block], table_send.at[k], table_recv.at[k], peer)
        for k, peer in enumerate(ori_peers)
    ]
    for copy in spreads:
        copy.start()
    start_near(1)
    start_far(0)
    start_near(2)
    start_far(1)
    start_near(3)
    start_far(2)
    for copy in spreads:
        copy.wait_recv()
    lane_row = lax.broadcasted_iota(jnp.int32, (LANES, LANES), 0)
    homes = [
        jnp.concatenate([tables[p * SIDE + z] for p in range(SIDE)], axis=0),
        jnp.concatenate([tables[x * SIDE + p] for p in range(SIDE)], axis=0),
    ]
    for d in range(SIDE):
        for s in range(SLOTS):
            for part, dest in enumerate((x * SIDE + ring(z, d), ring(x, d) * SIDE + z)):
                column = jnp.where(lane_row == s * BLOCKS + dest, 1.0, 0.0)
                pick = jnp.dot(homes[part], column, preferred_element_type=jnp.float32)
                for p in range(SIDE):
                    picks[part, d, s, p] = pick[p * PLANES : (p + 1) * PLANES]
    start_near(4)
    start_far(3)


    order = [(q, r) for q in range(BATCHES) for r in range(SIDE)]

    def fill(n):
        q, r = order[n]
        slot = n % AHEAD
        near_y, far_y = ring(y, ROUNDS[r][0]), ring(y, ROUNDS[r][1])

        def step(i, carry):
            cc, t = lax.div(i, 2), lax.rem(i, 2)
            m = (near_y + (far_y - near_y) * cc) * CORES + cc
            for part, (ref, place) in enumerate(((xa, z), (xb, x))):
                odd = lax.rem(place + q, 2)
                p = 2 * t + odd
                choices = [ref[p, m, g * group : (g + 1) * group, :] for g in range(groups)]
                for d in range(SIDE):
                    for s in range(SLOTS):
                        pick = jnp.broadcast_to(picks[part, d, s, p, pl.ds(m, 1), :], (group, LANES))
                        pick = jnp.concatenate([pick.astype(jnp.bfloat16)] * (half // LANES), axis=1)
                        value = choices[0]
                        for g in range(1, groups):
                            value = jnp.where(pick == g, choices[g], value)
                        if d and part == 0:
                            out_a[slot, d - 1, cc, s, t] = value
                        elif d:
                            out_b[slot, d - 1, cc, s, t] = value
                        elif part == 0:
                            arrived[q, r, cc, s, lax.div(z, 2), lax.rem(z, 2), t, :, 0:half] = value
                        else:
                            arrived[q, r, cc, s, t, odd, lax.div(x, 2), :, half : 2 * half] = value
            return carry

        lax.fori_loop(0, CORES * 2, step, 0)

    moves = {}

    def send(n):
        q, r = order[n]
        slot = n % AHEAD
        moves[n] = []
        for d in (2, 1, 3):
            moves[n].append(
                remote(
                    out_a.at[slot, d - 1],
                    arrived.at[q, r, :, :, lax.div(z, 2), lax.rem(z, 2), :, :, pl.ds(0, half)],
                    a_send.at[slot, d - 1],
                    a_recv.at[n, d - 1],
                    at_ori(x, ring(z, d)),
                )
            )
            moves[n].append(
                remote(
                    out_b.at[slot, d - 1],
                    arrived.at[q, r, :, :, :, lax.rem(x + q, 2), lax.div(x, 2), :, pl.ds(half, half)],
                    b_send.at[slot, d - 1],
                    b_recv.at[n, d - 1],
                    at_ori(ring(x, d), z),
                )
            )
        for copy in moves[n]:
            copy.start()

    start_near(5)
    start_far(4)
    wait_far(2)
    wait_far(3)
    fill(0)
    send(0)
    start_near(6)
    start_far(5)
    start_near(7)
    wait_far(4)
    wait_far(5)
    fill(1)
    send(1)
    start_far(6)
    start_far(7)
    for copy in tells + list(turns.values()) + spreads:
        copy.wait_send()
    load.wait()
    wide = proj[...].astype(jnp.float32)
    half_norm = 0.5 * jnp.sum(wide * wide, axis=1, keepdims=True)
    wait_far(6)
    wait_far(7)
    if AHEAD > 2:
        fill(2)
        send(2)
    wait_far(0)
    wait_far(1)

    def scores(q, r, cc):
        values = arrived[q, r, cc].reshape(lanes, slice_columns)
        return (
            lax.dot_general(proj[...], values, (((1,), (1,)), ((), ())), preferred_element_type=jnp.float32)
            - half_norm
        )

    pairs, sums = {}, {}

    def round_of(n):
        q, r = order[n]
        for copy in moves[n]:
            copy.wait_recv()
        if n + AHEAD < len(order):
            for copy in moves[n]:
                copy.wait_send()
            fill(n + AHEAD)
            send(n + AHEAD)
        slot = n % 2
        if n >= 2:
            pairs[n - 2].wait_send()
        pair_out[slot] = scores(q, r, other)
        pairs[n] = remote(pair_out.at[slot], pair_in.at[n], pair_send.at[slot], pair_recv.at[n], partner)
        pairs[n].start()
        kept[q, r] = scores(q, r, c)
        pairs[n].wait_recv()
        kept[q, r] += pair_in[n]
        if r < SIDE - 1:
            d = ROUNDS[r][0] + (ROUNDS[r][1] - ROUNDS[r][0]) * c
            sums[n] = remote(kept.at[q, r], y_in.at[q, d - 1], y_send.at[q, r], y_recv.at[q, d - 1], at_img(ring(y, d), c))
            sums[n].start()


    last = SIDE - 1
    shares = {}

    def share(q):
        for n in range(q * SIDE, q * SIDE + last):
            sums[n].wait_recv()
        kept[q, last] = kept[q, last] + y_in[q, 0] + y_in[q, 1] + y_in[q, 2]
        highest = jnp.max(kept[q, last], axis=0, keepdims=True)
        mass = jnp.sum(jnp.exp(kept[q, last] - highest), axis=0, keepdims=True)
        which = lax.broadcasted_iota(jnp.int32, (8, lanes), 0)
        stats[q, block] = jnp.where(which == 0, highest, mass)
        shares[q] = [
            remote(stats.at[q, block], stats.at[q, block], stat_send.at[q, k], stat_recv.at[q, k], peer)
            for k, peer in enumerate(ori_peers)
        ]
        for copy in shares[q]:
            copy.start()

    images_batch = lanes // SLOTS
    home_row = lax.broadcasted_iota(jnp.int32, (BLOCKS, images_batch), 0)
    home_lane = lax.broadcasted_iota(jnp.int32, (BLOCKS, images_batch), 1)
    lane_z, lane_t = lax.div(home_lane, 2 * group), lax.rem(lax.div(home_lane, group), 2)
    block_row = lax.broadcasted_iota(jnp.int32, (BLOCKS, lanes), 0)

    def respond(q):
        spot = (2 * lane_t + lax.rem(lane_z + q, 2)) * SIDE + lane_z
        widen = jnp.where(home_row == spot, 1.0, 0.0)
        plane = tables[:, pl.ds(me, 1), :].reshape(BLOCKS, LANES)
        named = lax.dot_general(plane, widen, (((0,), (0,)), ((), ())), preferred_element_type=jnp.float32)
        named = jnp.concatenate([named[s * BLOCKS : (s + 1) * BLOCKS] for s in range(SLOTS)], axis=1)
        own = jnp.sum(jnp.where(block_row == block, named, 0.0), axis=0, keepdims=True)
        for copy in shares[q]:
            copy.wait()
        tops, masses = stats[q, :, 0, :], stats[q, :, 1, :]
        norm = jnp.zeros((1, lanes), jnp.float32)
        for g in range(groups):
            listed = named == g
            top = jnp.max(jnp.where(listed, tops, NO_SCORE), axis=0, keepdims=True)
            top = jnp.maximum(top[:, :images_batch], top[:, images_batch:])
            top2 = jnp.concatenate([top, top], axis=1)
            mass = jnp.where(listed, jnp.exp(jnp.minimum(tops - top2, 0.0)) * masses, 0.0)
            mass = jnp.sum(mass, axis=0, keepdims=True)
            value = top + jnp.log(mass[:, :images_batch] + mass[:, images_batch:])
            loglik[q, pl.ds(g, 1), :] = value
            norm = jnp.where(own == g, jnp.concatenate([value, value], axis=1), norm)
        value = jnp.where(own >= 0, jnp.exp(kept[q, last] - norm), 0.0).astype(jnp.bfloat16)
        for h in range(2):
            resp[q, 0, c, h] = value[:, h * LANES : (h + 1) * LANES]


    direct, passed, crossed = {}, {}, {}

    def cross(q, d):
        crossed[q, d] = remote(resp.at[q, d, c], resp.at[q, d, c], rc_send.at[q, d], rc_recv.at[q, d], partner)
        crossed[q, d].start()

    def gather_near(q):
        for step in range(2):
            for d, h in ((1, step), (3, 1 - step)):
                direct[q, d, h] = remote(
                    resp.at[q, 0, c, h], resp.at[q, d, c, h], r_send.at[q, d, h], r_recv.at[q, d, h], at_img(ring(y, -d), c)
                )
                direct[q, d, h].start()
        cross(q, 0)

    def gather_far(q):
        for d, h in ((1, 0), (3, 1)):
            direct[q, d, h].wait_recv()
            passed[q, h] = remote(
                resp.at[q, d, c, h], resp.at[q, 2, c, h], r_send.at[q, 2, h], r_recv.at[q, 2, h], at_img(ring(y, -d), c)
            )
            passed[q, h].start()
        for d, h in ((1, 1), (3, 0)):
            direct[q, d, h].wait_recv()
            cross(q, d)

    def gather_last(q):
        for h in range(2):
            passed[q, h].wait_recv()
        cross(q, 2)

    tile = 2 * LANES

    def add(q, d, first=False, final=False):
        crossed[q, d].wait_recv()
        for t in range(slice_columns // tile):
            cols = slice(t * tile, (t + 1) * tile)
            part = None if first else total[:, cols]
            for cc in range(CORES):
                r = [pair[cc] for pair in ROUNDS].index(d)
                factor = jnp.concatenate([resp[q, d, cc, 0], resp[q, d, cc, 1]], axis=1)
                values = arrived[q, r, cc, :, :, :, :, :, cols].reshape(lanes, tile)
                product = jnp.dot(factor, values, preferred_element_type=jnp.float32)
                part = product if part is None else part + product
            if final:
                weighted[:, cols] = part.astype(weighted.dtype)
            else:
                total[:, cols] = part

    for n in range(4):
        round_of(n)
    share(0)
    round_of(4)
    respond(0)
    gather_near(0)
    round_of(5)
    gather_far(0)
    add(0, 0, first=True)
    round_of(6)
    gather_last(0)
    add(0, 1)
    round_of(7)
    share(1)
    add(0, 3)
    add(0, 2)
    respond(1)
    gather_near(1)
    add(1, 0)
    gather_far(1)
    add(1, 1)
    add(1, 3)
    gather_last(1)
    add(1, 2, final=True)

    for copy in list(near.values()) + list(far.values()):
        copy.wait_send()
    for n in range(len(order) - AHEAD, len(order)):
        for copy in moves[n]:
            copy.wait_send()
    for n in (len(order) - 2, len(order) - 1):
        pairs[n].wait_send()
    for copies in (sums, direct, passed, crossed):
        for copy in copies.values():
            copy.wait_send()


def per_device(images, projections, search):
    groups, _ = search.shape
    rows, columns = images.shape
    group = rows // groups
    slice_columns = columns // PLANES
    half = slice_columns // 2
    oris = projections.shape[0]
    lanes = BLOCKS * SLOTS * group // BATCHES
    peers, rounds = SIDE - 1, BATCHES * SIDE

    vmem, anywhere = pl.BlockSpec(memory_space=pltpu.VMEM), pl.BlockSpec(memory_space=pl.ANY)
    bf16, f32, dma = jnp.bfloat16, jnp.float32, pltpu.SemaphoreType.DMA
    weighted, loglik = pl.pallas_call(
        kernel,
        out_shape=(
            jax.ShapeDtypeStruct((oris, slice_columns), bf16),
            jax.ShapeDtypeStruct((BATCHES, groups, lanes // SLOTS), f32),
        ),
        in_specs=[pl.BlockSpec(memory_space=pltpu.SMEM), anywhere, anywhere],
        out_specs=(vmem, vmem),
        scratch_shapes=[
            pltpu.VMEM((SIDE, PLANES, rows, half), bf16),
            pltpu.VMEM((SIDE, PLANES, rows, half), bf16),
            pltpu.VMEM((PLANES, 8, LANES), f32),
            pltpu.VMEM((BLOCKS, PLANES, LANES), f32),
            pltpu.VMEM((2, SIDE, SLOTS, SIDE, PLANES, LANES), f32),
            pltpu.VMEM((oris, slice_columns), bf16),
            pltpu.VMEM((BATCHES, SIDE, CORES, SLOTS, 2, 2, 2, group, slice_columns), bf16),
            pltpu.VMEM((AHEAD, peers, CORES, SLOTS, 2, group, half), bf16),
            pltpu.VMEM((AHEAD, peers, CORES, SLOTS, 2, group, half), bf16),
            pltpu.VMEM((2, oris, lanes), f32),
            pltpu.VMEM((rounds, oris, lanes), f32),
            pltpu.VMEM((BATCHES, SIDE, oris, lanes), f32),
            pltpu.VMEM((BATCHES, peers, oris, lanes), f32),
            pltpu.VMEM((BATCHES, BLOCKS, 8, lanes), f32),
            pltpu.VMEM((BATCHES, SIDE, CORES, 2, oris, LANES), bf16),
            pltpu.VMEM((oris, slice_columns), f32),
            dma((3,)),
            dma((PLANES - 1, 2)),
            dma((SIDE, CORES, 2)),
            dma((PLANES - 1,)),
            dma((SIDE, CORES)),
            dma((BLOCKS - 1,)),
            dma((BLOCKS - 1,)),
            dma((PLANES, 4)),
            dma((PLANES, 4)),
            dma((PLANES, 4)),
            dma((PLANES, 4)),
            dma((AHEAD, peers)),
            dma((rounds, peers)),
            dma((AHEAD, peers)),
            dma((rounds, peers)),
            dma((2,)),
            dma((rounds,)),
            dma((BATCHES, peers)),
            dma((BATCHES, peers)),
            dma((BATCHES, BLOCKS - 1)),
            dma((BATCHES, BLOCKS - 1)),
            dma((BATCHES, SIDE, 2)),
            dma((BATCHES, SIDE, 2)),
            dma((BATCHES, SIDE)),
            dma((BATCHES, SIDE)),
        ],
        compiler_params=pltpu.CompilerParams(collective_id=0, has_side_effects=True, vmem_limit_bytes=62 * 2**20),
        cost_estimate=pl.CostEstimate(flops=15 * 10**9, bytes_accessed=32 * 2**20, transcendentals=10**6),
    )(search, images, projections)
    b = lax.axis_index("ori")
    x, z = lax.div(b, SIDE), lax.rem(b, SIDE)
    start = z * (2 * group) + lax.div(x, 2) * group
    loglik = lax.dynamic_slice(loglik, (lax.rem(x + z, BATCHES), 0, start), (1, groups, group))
    return weighted, loglik.reshape(-1)


def solution(mesh):
    placed = (P(("img", "ori"), None), P("ori", None), P(("img", "ori"), None))
    return jax.shard_map(
        per_device,
        mesh=mesh,
        in_specs=placed,
        out_specs=(P("ori", "img"), P(("img", "ori"))),
        check_vma=False,
    )
```

```python
import jax
import jax.numpy as jnp
from jax import lax
from jax.experimental import pallas as pl
from jax.experimental.pallas import tpu as pltpu
from jax.sharding import PartitionSpec as P

MESH = pl.DeviceIdType.MESH
SIDE = 4
CORES = 2
PLANES = SIDE * CORES
BLOCKS = SIDE * SIDE
SLOTS = 2
LANES = 128
BATCHES = SIDE
AHEAD = 3
NO_SCORE = -3.0e38

ROUNDS = [(2, 2), (1, 3), (3, 1), (0, 0)]
ORDER = [(0, 3), (0, 1), (0, 2), (1, 3), (0, 0), (1, 0), (1, 1), (1, 2)] + [(q, r) for q in (2, 3) for r in range(4)]
RELAYED = (1, 2, 3)


def ring(position, step):
    return lax.rem(position + step + SIDE, SIDE)


def at_img(y, c):
    return {"img": y * CORES + c, "ori": lax.axis_index("ori")}


def at_ori(x, z):
    return {"img": lax.axis_index("img"), "ori": x * SIDE + z}


def remote(source, target, send, recv, device):
    return pltpu.make_async_remote_copy(
        src_ref=source,
        dst_ref=target,
        send_sem=send,
        recv_sem=recv,
        device_id=device,
        device_id_type=MESH,
    )


def greet(devices):
    barrier = pltpu.get_barrier_semaphore()
    for device in devices:
        pl.semaphore_signal(barrier, inc=1, device_id=device, device_id_type=MESH)
    pl.semaphore_wait(barrier, len(devices))


def slot_table(search):
    lane = lax.broadcasted_iota(jnp.int32, (8, LANES), 1)
    b, s = lax.rem(lane, BLOCKS), lax.div(lane, BLOCKS)
    table = jnp.full((8, LANES), -1.0, jnp.float32)
    rank = jnp.zeros((8, LANES), jnp.int32)
    for g in range(search.shape[0]):
        hit = b == search[g, 0]
        for n in range(1, search.shape[1]):
            hit = hit | (b == search[g, n])
        table = jnp.where(hit & (rank == s), float(g), table)
        rank = rank + hit.astype(jnp.int32)
    return table


def kernel(
    search,
    images,
    projections,
    weighted,
    loglik,
    xa,
    xb,
    told,
    tables,
    picks,
    proj,
    arrived,
    out_a,
    out_b,
    pair_out,
    pair_in,
    kept,
    y_half,
    y_in,
    stats,
    resp,
    scale,
    result,
    total,
    load_sem,
    turn_send,
    turn_recv,
    told_send,
    told_recv,
    table_send,
    table_recv,
    near_send,
    near_recv,
    far_send,
    far_recv,
    a_send,
    a_recv,
    b_send,
    b_recv,
    pair_send,
    pair_recv,
    h_send,
    h_recv,
    y_send,
    y_recv,
    stat_send,
    stat_recv,
    r_send,
    r_recv,
    rc_send,
    rc_recv,
    f_send,
    f_recv,
):
    me, block = lax.axis_index("img"), lax.axis_index("ori")
    y, c = lax.div(me, CORES), lax.rem(me, CORES)
    x, z = lax.div(block, SIDE), lax.rem(block, SIDE)
    other = 1 - c
    rows, half = xa.shape[2], xa.shape[3]
    mid = rows // 2
    group = arrived.shape[5]
    groups = rows // group
    slice_columns = 2 * half
    lanes = kept.shape[3]
    partner = at_img(y, other)
    steps = [(dx, dz) for dx in range(SIDE) for dz in range(SIDE) if (dx, dz) != (0, 0)]
    ori_peers = [at_ori(ring(x, dx), ring(z, dz)) for dx, dz in steps]
    img_peers = [partner] + [at_img(ring(y, d), cc) for d in range(1, SIDE) for cc in range(CORES)]
    neighbours = [at_ori(ring(x, 1), z), at_ori(ring(x, -1), z), at_ori(x, ring(z, 1)), at_ori(x, ring(z, -1))]


    def columns(m, part):
        return images.at[:, pl.ds(pl.multiple_of(m * slice_columns + part * half, LANES), half)]

    def line(part):
        return (xa, x) if part == 0 else (xb, z)

    home = []
    for part in range(2):
        ref, place = line(part)
        home.append(pltpu.make_async_copy(columns(me, part), ref.at[place, me], load_sem.at[part]))
    load = pltpu.make_async_copy(
        projections.at[:, pl.ds(pl.multiple_of(me * slice_columns, LANES), slice_columns)], proj, load_sem.at[2]
    )
    for copy in home + [load]:
        copy.start()
    told[me] = slot_table(search)
    greet(img_peers + ori_peers)
    receivers = [(0, other)] + [(d, cc) for d in (1 + 2 * c, 3 - 2 * c, 2) for cc in range(CORES)]
    tells, turns = [], {}
    for k, (d, cc) in enumerate(receivers):
        tells.append(remote(told.at[me], told.at[me], told_send.at[k], told_recv.at[d, c], at_img(ring(y, -d), cc)))
        tells[-1].start()

    def turn(ks):
        for k in ks:
            d, cc = receivers[k]
            for part in range(2):
                ref, place = line(part)
                turns[k, part] = remote(
                    columns(ring(y, -d) * CORES + cc, part),
                    ref.at[place, me],
                    turn_send.at[k, part],
                    turn_recv.at[d, c, part],
                    at_img(ring(y, -d), cc),
                )
                turns[k, part].start()

    turn(range(PLANES - 1))

    sources = [(0, c), (0, other), (1, 0), (3, 1), (3, 0), (1, 1), (2, 0), (2, 1)]

    def source(k):
        d, cc = sources[k]
        return ring(y, d) * CORES + cc

    near, far = {}, {}

    def start_near(k):
        d, cc = sources[k]
        for part in range(2):
            ref, place = line(part)
            block_ref = ref.at[place, source(k)]
            if k == 0:
                home[part].wait()
            else:
                remote(
                    block_ref, block_ref, turn_send.at[k - 1, part], turn_recv.at[d, cc, part], partner
                ).wait_recv()
            for way in (2 * part, 2 * part + 1):
                near[k, way] = remote(
                    block_ref, block_ref, near_send.at[k, way], near_recv.at[k, way], neighbours[way]
                )
                near[k, way].start()

    def start_far(k):
        for way in range(4):
            ref, place = line(way // 2)
            forward = way % 2 == 0
            near[k, way].wait_recv()
            block_ref = ref.at[ring(place, -1 if forward else 1), source(k), pl.ds(0 if forward else mid, mid)]
            far[k, way] = remote(block_ref, block_ref, far_send.at[k, way], far_recv.at[k, way], neighbours[way])
            far[k, way].start()

    def wait_far(k):
        for way in range(4):
            far[k, way].wait_recv()

    start_near(0)
    for d in range(SIDE):
        for cc in range(CORES) if d else (other,):
            tile = told.at[ring(y, d) * CORES + cc]
            remote(tile, tile, told_send.at[0], told_recv.at[d, cc], partner).wait_recv()
    sublane = lax.broadcasted_iota(jnp.int32, (PLANES, LANES), 0)
    gathered = told[0]
    for m in range(1, PLANES):
        gathered = jnp.where(sublane == m, told[m], gathered)
    tables[block] = gathered
    spreads = [
        remote(tables.at[block], tables.at[block], table_send.at[k], table_recv.at[k], peer)
        for k, peer in enumerate(ori_peers)
    ]
    for copy in spreads:
        copy.start()
    start_near(1)
    start_far(0)
    start_far(1)
    for copy in spreads:
        copy.wait_recv()
    lane_row = lax.broadcasted_iota(jnp.int32, (LANES, LANES), 0)
    homes = [
        jnp.concatenate([tables[p * SIDE + z] for p in range(SIDE)], axis=0),
        jnp.concatenate([tables[x * SIDE + p] for p in range(SIDE)], axis=0),
    ]
    for d in range(SIDE):
        for s in range(SLOTS):
            for part, dest in enumerate((x * SIDE + ring(z, d), ring(x, d) * SIDE + z)):
                column = jnp.where(lane_row == s * BLOCKS + dest, 1.0, 0.0)
                pick = jnp.dot(homes[part], column, preferred_element_type=jnp.float32)
                for p in range(SIDE):
                    picks[part, d, s, p] = pick[p * PLANES : (p + 1) * PLANES]


    order = ORDER

    def fill(n):
        q, r = order[n]
        slot = n % AHEAD
        ys = [ring(y, d) for d in ROUNDS[r]]

        def step(cc, carry):
            m = (ys[0] + (ys[1] - ys[0]) * cc) * CORES + cc
            for part, (ref, place) in enumerate(((xa, z), (xb, x))):
                p = ring(q, -place)
                choices = [ref[p, m, g * group : (g + 1) * group, :] for g in range(groups)]
                for d in range(SIDE):
                    for s in range(SLOTS):
                        pick = jnp.broadcast_to(picks[part, d, s, p, pl.ds(m, 1), :], (group, LANES))
                        pick = jnp.concatenate([pick.astype(jnp.bfloat16)] * (half // LANES), axis=1)
                        value = choices[0]
                        for g in range(1, groups):
                            value = jnp.where(pick == g, choices[g], value)
                        if d and part == 0:
                            out_a[slot, d - 1, cc, s] = value
                        elif d:
                            out_b[slot, d - 1, cc, s] = value
                        elif part == 0:
                            arrived[q, r, cc, s, z, :, 0:half] = value
                        else:
                            arrived[q, r, cc, s, p, :, half : 2 * half] = value
            return carry

        lax.fori_loop(0, CORES, step, 0)

    moves = {}

    def send(n):
        q, r = order[n]
        slot = n % AHEAD
        moves[n] = []
        for d in (2, 1, 3):
            moves[n].append(
                remote(
                    out_a.at[slot, d - 1],
                    arrived.at[q, r, :, :, z, :, pl.ds(0, half)],
                    a_send.at[slot, d - 1],
                    a_recv.at[n, d - 1],
                    at_ori(x, ring(z, d)),
                )
            )
            moves[n].append(
                remote(
                    out_b.at[slot, d - 1],
                    arrived.at[q, r, :, :, ring(q, -x), :, pl.ds(half, half)],
                    b_send.at[slot, d - 1],
                    b_recv.at[n, d - 1],
                    at_ori(ring(x, d), z),
                )
            )
        for copy in moves[n]:
            copy.start()

    wait_far(0)
    wait_far(1)
    fill(0)
    send(0)
    for k in range(2, 6):
        start_near(k)
    start_far(2)
    start_far(3)
    start_near(6)
    start_near(7)
    start_far(4)
    start_far(5)
    wait_far(2)
    wait_far(3)
    fill(1)
    send(1)
    start_far(6)
    start_far(7)
    wait_far(4)
    wait_far(5)
    fill(2)
    send(2)
    for copy in tells + list(turns.values()) + spreads:
        copy.wait_send()
    load.wait()
    wide = proj[...].astype(jnp.float32)
    half_norm = 0.5 * jnp.sum(wide * wide, axis=1, keepdims=True)


    pairs, sums, thirds = {}, {}, {}
    last = SIDE - 1
    mid_ori = kept.shape[2] // 2

    def refill(n):
        for copy in moves[n]:
            copy.wait_send()
        fill(n + AHEAD)
        send(n + AHEAD)

    def begin(n):
        q, r = order[n]
        slot = n % 2
        if n >= 2:
            pairs[n - 2].wait_send()
        values = arrived[q, r].reshape(CORES * lanes, slice_columns)
        value = lax.dot_general(proj[...], values, (((1,), (1,)), ((), ())), preferred_element_type=jnp.float32)
        value = value - half_norm
        for cc in range(CORES):
            pair_out[slot, cc] = value[:, cc * lanes : (cc + 1) * lanes]
        pairs[n] = remote(pair_out.at[slot, other], pair_in.at[n], pair_send.at[slot], pair_recv.at[n], partner)
        pairs[n].start()

    def finish(n):
        q, r = order[n]
        pairs[n].wait_recv()
        kept[q, r] = pair_out[n % 2, c] + pair_in[n]
        if r == 0 and q in RELAYED:
            for h, step in ((0, 1), (1, -1)):
                rows_h = pl.ds(h * mid_ori, mid_ori)
                thirds[q, h] = remote(
                    kept.at[q, r, rows_h], y_half.at[q, h], h_send.at[q, h], h_recv.at[q, h], at_img(ring(y, step), c)
                )
                thirds[q, h].start()
        elif r == 0:
            sums[n] = remote(kept.at[q, r], y_in.at[q, 2], y_send.at[q, 2], y_recv.at[q, 2], at_img(ring(y, 2), c))
            sums[n].start()
        elif r < last and q not in RELAYED:
            pass_on(n)

    def pass_on(n):
        q, r = order[n]
        d0, d1 = ROUNDS[r]
        d = d0 + (d1 - d0) * c
        h = lax.div(d, 2)
        if q in RELAYED:
            half_ref = y_half.at[q, h]
            remote(half_ref, half_ref, h_send.at[q, h], h_recv.at[q, h], partner).wait_recv()
            rows_h = pl.ds(pl.multiple_of(h * mid_ori, 8), mid_ori)
            kept[q, r, rows_h, :] = kept[q, r, rows_h, :] + y_half[q, h]
        sums[n] = remote(kept.at[q, r], y_in.at[q, h], y_send.at[q, h], y_recv.at[q, h], at_img(ring(y, d), c))
        sums[n].start()


    shares = {}

    def share(q):
        for n, copy in sums.items():
            if order[n][0] == q:
                copy.wait_recv()
        value = kept[q, last] + y_in[q, 0] + y_in[q, 1]
        if q not in RELAYED:
            value = value + y_in[q, 2]
        kept[q, last] = value
        highest = jnp.max(kept[q, last], axis=0, keepdims=True)
        value = jnp.exp(kept[q, last] - highest)
        resp[q, 0, c] = value.astype(jnp.bfloat16)
        mass = jnp.sum(value, axis=0, keepdims=True)
        which = lax.broadcasted_iota(jnp.int32, (8, lanes), 0)
        stats[q, block] = jnp.where(which == 0, highest, mass)
        shares[q] = [
            remote(stats.at[q, block], stats.at[q, block], stat_send.at[q, k], stat_recv.at[q, k], peer)
            for k, peer in enumerate(ori_peers)
        ]
        for copy in shares[q]:
            copy.start()

    images_batch = lanes // SLOTS
    home_row = lax.broadcasted_iota(jnp.int32, (BLOCKS, lanes), 0)
    home_lane = lax.broadcasted_iota(jnp.int32, (BLOCKS, lanes), 1)
    lane_z = lax.rem(lax.div(home_lane, group), SIDE)

    here = lax.rem(x + z, BATCHES)
    lane = lax.broadcasted_iota(jnp.int32, (1, lanes), 1)
    factors = {}

    def fold(value, operation):
        return operation(value, pltpu.roll(value, images_batch, 1))

    def respond(q):
        spot = lax.rem(q - lane_z + SIDE, SIDE) * SIDE + lane_z
        widen = jnp.where(home_row == spot, 1.0, 0.0)
        plane = tables[:, pl.ds(me, 1), :].reshape(BLOCKS, LANES)
        named = lax.dot_general(plane, widen, (((0,), (0,)), ((), ())), preferred_element_type=jnp.float32)
        named = jnp.where(home_lane < images_batch, named[:BLOCKS], named[BLOCKS : 2 * BLOCKS])
        own = jnp.sum(jnp.where(home_row == block, named, 0.0), axis=0, keepdims=True)
        for copy in shares[q]:
            copy.wait()
        tops, masses = stats[q, :, 0, :], stats[q, :, 1, :]
        norm = jnp.zeros((1, lanes), jnp.float32)
        row = jnp.zeros((1, lanes), jnp.float32) if q == 0 else result[...]
        for g in range(groups):
            listed = named == g
            top = fold(jnp.max(jnp.where(listed, tops, NO_SCORE), axis=0, keepdims=True), jnp.maximum)
            mass = jnp.where(listed, jnp.exp(jnp.minimum(tops - top, 0.0)) * masses, 0.0)
            mass = fold(jnp.sum(mass, axis=0, keepdims=True), jnp.add)
            value = top + jnp.log(mass)
            moved = pltpu.roll(value, lax.rem((g - z) * group + lanes, lanes), 1)
            row = jnp.where((lax.div(lane, group) == g) & (here == q), moved, row)
            norm = jnp.where(own == g, value, norm)
        result[...] = row
        value = jnp.where(own >= 0, jnp.exp(stats[q, pl.ds(block, 1), 0, :] - norm), 0.0)
        scale[q, 0, c] = jnp.broadcast_to(value, (8, lanes))
        factors[q] = []
        for k, (d, cc) in enumerate(receivers):
            factors[q].append(
                remote(
                    scale.at[q, 0, c], scale.at[q, d, c], f_send.at[q, k], f_recv.at[q, d, c], at_img(ring(y, -d), cc)
                )
            )
            factors[q][-1].start()


    direct, passed, crossed = {}, {}, {}

    def cross(q, d):
        crossed[q, d] = remote(resp.at[q, d, c], resp.at[q, d, c], rc_send.at[q, d], rc_recv.at[q, d], partner)
        crossed[q, d].start()

    def part_of(q, d, h):
        return resp.at[q, d, c, pl.ds(h * mid_ori, mid_ori)]

    def gather_near(q):
        cross(q, 0)
        for step in range(2):
            for d, h in ((1, step), (3, 1 - step)):
                direct[q, d, h] = remote(
                    part_of(q, 0, h), part_of(q, d, h), r_send.at[q, d, h], r_recv.at[q, d, h], at_img(ring(y, -d), c)
                )
                direct[q, d, h].start()

    def gather_direct(q):
        cross(q, 0)
        for d in (2, 1, 3):
            direct[q, d] = remote(
                resp.at[q, 0, c], resp.at[q, d, c], r_send.at[q, d, 0], r_recv.at[q, d, 0], at_img(ring(y, -d), c)
            )
            direct[q, d].start()

    def gather_far(q):
        for d, h in ((1, 0), (3, 1)):
            direct[q, d, h].wait_recv()
            passed[q, h] = remote(
                part_of(q, d, h), part_of(q, 2, h), r_send.at[q, 2, h], r_recv.at[q, 2, h], at_img(ring(y, -d), c)
            )
            passed[q, h].start()
        for d, h in ((1, 1), (3, 0)):
            direct[q, d, h].wait_recv()
            cross(q, d)

    def gather_last(q):
        for h in range(2):
            passed[q, h].wait_recv()
        cross(q, 2)

    tile = 2 * LANES

    def add(q, ds):
        for d in ds:
            crossed[q, d].wait_recv()
            for cc in range(CORES) if d else (other,):
                ref = scale.at[q, d, cc]
                remote(ref, ref, f_send.at[q, 0], f_recv.at[q, d, cc], partner).wait_recv()
        first, final = q == 0, q == BATCHES - 1 and 2 in ds
        pieces = [(d, cc) for d in ds for cc in range(CORES)]
        factor = jnp.concatenate(
            [(resp[q, d, cc].astype(jnp.float32) * scale[q, d, cc, 0:1, :]).astype(jnp.bfloat16) for d, cc in pieces], axis=1
        )
        for t in range(slice_columns // tile):
            cols = slice(t * tile, (t + 1) * tile)
            values = []
            for d, cc in pieces:
                r = [pair[cc] for pair in ROUNDS].index(d)
                values.append(arrived[q, r, cc, :, :, :, cols].reshape(lanes, tile))
            part = jnp.dot(factor, jnp.concatenate(values, axis=0), preferred_element_type=jnp.float32)
            if not first:
                part = part + total[:, cols]
            if final:
                weighted[:, cols] = part.astype(weighted.dtype)
            else:
                total[:, cols] = part

    shares_at, passes_at = {8: 0, 11: 1, 15: 2}, {8: (6, 7), 11: (9, 10), 13: (13,), 14: (14,)}
    for n in range(len(order)):
        for copy in moves[n]:
            copy.wait_recv()
        if n in shares_at:
            share(shares_at[n])
            gather_near(shares_at[n])
        if n == 1:
            wait_far(6)
            wait_far(7)
        if n + AHEAD < len(order):
            refill(n)
        begin(n)
        if 0 < n <= 12:
            finish(n - 1)
        if n >= 12:
            finish(n)
        for k in passes_at.get(n, ()):
            pass_on(k)
        if n == 9:
            gather_far(0)
        if n == 10:
            respond(0)
        if n == 11:
            gather_last(0)
        if n == 13:
            add(0, range(SIDE))
            gather_far(1)
        if n == 14:
            respond(1)
    gather_far(2)
    share(3)
    gather_direct(3)
    gather_last(1)
    add(1, range(SIDE))
    respond(2)
    gather_last(2)
    respond(3)
    add(2, range(SIDE))
    for d in (1, 3):
        direct[3, d].wait_recv()
        cross(3, d)
    add(3, (0, 1, 3))
    direct[3, 2].wait_recv()
    cross(3, 2)
    add(3, (2,))
    loglik[...] = result[:, 0 : loglik.shape[1]]

    for copy in list(near.values()) + list(far.values()):
        copy.wait_send()
    for n in range(len(order) - AHEAD, len(order)):
        for copy in moves[n]:
            copy.wait_send()
    for n in (len(order) - 2, len(order) - 1):
        pairs[n].wait_send()
    for q in range(BATCHES):
        for copy in factors[q]:
            copy.wait_send()
    for copies in (sums, thirds, direct, passed, crossed):
        for copy in copies.values():
            copy.wait_send()


def per_device(images, projections, search):
    groups, _ = search.shape
    rows, columns = images.shape
    group = rows // groups
    slice_columns = columns // PLANES
    half = slice_columns // 2
    oris = projections.shape[0]
    lanes = BLOCKS * SLOTS * group // BATCHES
    peers, rounds = SIDE - 1, BATCHES * SIDE
    mid_ori = oris // 2

    vmem, anywhere = pl.BlockSpec(memory_space=pltpu.VMEM), pl.BlockSpec(memory_space=pl.ANY)
    bf16, f32, dma = jnp.bfloat16, jnp.float32, pltpu.SemaphoreType.DMA
    weighted, loglik = pl.pallas_call(
        kernel,
        out_shape=(
            jax.ShapeDtypeStruct((oris, slice_columns), bf16),
            jax.ShapeDtypeStruct((1, rows), f32),
        ),
        in_specs=[pl.BlockSpec(memory_space=pltpu.SMEM), anywhere, anywhere],
        out_specs=(vmem, vmem),
        scratch_shapes=[
            pltpu.VMEM((SIDE, PLANES, rows, half), bf16),
            pltpu.VMEM((SIDE, PLANES, rows, half), bf16),
            pltpu.VMEM((PLANES, 8, LANES), f32),
            pltpu.VMEM((BLOCKS, PLANES, LANES), f32),
            pltpu.VMEM((2, SIDE, SLOTS, SIDE, PLANES, LANES), f32),
            pltpu.VMEM((oris, slice_columns), bf16),
            pltpu.VMEM((BATCHES, SIDE, CORES, SLOTS, SIDE, group, slice_columns), bf16),
            pltpu.VMEM((AHEAD, peers, CORES, SLOTS, group, half), bf16),
            pltpu.VMEM((AHEAD, peers, CORES, SLOTS, group, half), bf16),
            pltpu.VMEM((2, CORES, oris, lanes), f32),
            pltpu.VMEM((rounds, oris, lanes), f32),
            pltpu.VMEM((BATCHES, SIDE, oris, lanes), f32),
            pltpu.VMEM((BATCHES, 2, mid_ori, lanes), f32),
            pltpu.VMEM((BATCHES, peers, oris, lanes), f32),
            pltpu.VMEM((BATCHES, BLOCKS, 8, lanes), f32),
            pltpu.VMEM((BATCHES, SIDE, CORES, oris, lanes), bf16),
            pltpu.VMEM((BATCHES, SIDE, CORES, 8, lanes), f32),
            pltpu.VMEM((1, lanes), f32),
            pltpu.VMEM((oris, slice_columns), f32),
            dma((3,)),
            dma((PLANES - 1, 2)),
            dma((SIDE, CORES, 2)),
            dma((PLANES - 1,)),
            dma((SIDE, CORES)),
            dma((BLOCKS - 1,)),
            dma((BLOCKS - 1,)),
            dma((PLANES, 4)),
            dma((PLANES, 4)),
            dma((PLANES, 4)),
            dma((PLANES, 4)),
            dma((AHEAD, peers)),
            dma((rounds, peers)),
            dma((AHEAD, peers)),
            dma((rounds, peers)),
            dma((2,)),
            dma((rounds,)),
            dma((BATCHES, 2)),
            dma((BATCHES, 2)),
            dma((BATCHES, peers)),
            dma((BATCHES, peers)),
            dma((BATCHES, BLOCKS - 1)),
            dma((BATCHES, BLOCKS - 1)),
            dma((BATCHES, SIDE, 2)),
            dma((BATCHES, SIDE, 2)),
            dma((BATCHES, SIDE)),
            dma((BATCHES, SIDE)),
            dma((BATCHES, PLANES - 1)),
            dma((BATCHES, SIDE, CORES)),
        ],
        compiler_params=pltpu.CompilerParams(collective_id=0, has_side_effects=True, vmem_limit_bytes=62 * 2**20),
        cost_estimate=pl.CostEstimate(flops=15 * 10**9, bytes_accessed=32 * 2**20, transcendentals=10**6),
    )(search, images, projections)
    return weighted, loglik.reshape(-1)


def solution(mesh):
    placed = (P(("img", "ori"), None), P("ori", None), P(("img", "ori"), None))
    return jax.shard_map(
        per_device,
        mesh=mesh,
        in_specs=placed,
        out_specs=(P("ori", "img"), P(("img", "ori"))),
        check_vma=False,
    )
```

```python
import jax
import jax.numpy as jnp
from jax import lax
from jax.experimental import pallas as pl
from jax.experimental.pallas import tpu as pltpu
from jax.sharding import PartitionSpec as P

MESH = pl.DeviceIdType.MESH
SIDE = 4
CORES = 2
PLANES = SIDE * CORES
BLOCKS = SIDE * SIDE
SLOTS = 2
LANES = 128
BATCHES = SIDE
AHEAD = 3
NO_SCORE = -3.0e38

ROUNDS = [(2, 2), (1, 3), (3, 1), (0, 0)]
ORDER = [(0, 3), (0, 1), (0, 2), (1, 3), (0, 0), (1, 0), (1, 1), (1, 2)]
ORDER += [(2, 0), (2, 1), (2, 2), (3, 0), (3, 1), (3, 2), (2, 3), (3, 3)]
RELAYED = (1, 2, 3)


def ring(position, step):
    return lax.rem(position + step + SIDE, SIDE)


def at_img(y, c):
    return {"img": y * CORES + c, "ori": lax.axis_index("ori")}


def at_ori(x, z):
    return {"img": lax.axis_index("img"), "ori": x * SIDE + z}


def remote(source, target, send, recv, device):
    return pltpu.make_async_remote_copy(
        src_ref=source,
        dst_ref=target,
        send_sem=send,
        recv_sem=recv,
        device_id=device,
        device_id_type=MESH,
    )


def greet(devices):
    barrier = pltpu.get_barrier_semaphore()
    for device in devices:
        pl.semaphore_signal(barrier, inc=1, device_id=device, device_id_type=MESH)
    pl.semaphore_wait(barrier, len(devices))


def slot_table(search):
    lane = lax.broadcasted_iota(jnp.int32, (8, LANES), 1)
    b, s = lax.rem(lane, BLOCKS), lax.div(lane, BLOCKS)
    table = jnp.full((8, LANES), -1.0, jnp.float32)
    rank = jnp.zeros((8, LANES), jnp.int32)
    for g in range(search.shape[0]):
        hit = b == search[g, 0]
        for n in range(1, search.shape[1]):
            hit = hit | (b == search[g, n])
        table = jnp.where(hit & (rank == s), float(g), table)
        rank = rank + hit.astype(jnp.int32)
    return table


def kernel(
    search,
    images,
    projections,
    weighted,
    loglik,
    xa,
    xb,
    told,
    tables,
    picks,
    proj,
    arrived,
    out_a,
    out_b,
    pair_out,
    pair_in,
    kept,
    y_half,
    y_in,
    stats,
    resp,
    scale,
    result,
    total,
    load_sem,
    turn_send,
    turn_recv,
    told_send,
    told_recv,
    table_send,
    table_recv,
    near_send,
    near_recv,
    far_send,
    far_recv,
    a_send,
    a_recv,
    b_send,
    b_recv,
    pair_send,
    pair_recv,
    h_send,
    h_recv,
    y_send,
    y_recv,
    stat_send,
    stat_recv,
    r_send,
    r_recv,
    rc_send,
    rc_recv,
    f_send,
    f_recv,
):
    me, block = lax.axis_index("img"), lax.axis_index("ori")
    y, c = lax.div(me, CORES), lax.rem(me, CORES)
    x, z = lax.div(block, SIDE), lax.rem(block, SIDE)
    other = 1 - c
    rows, half = xa.shape[2], xa.shape[3]
    mid = rows // 2
    group = arrived.shape[5]
    groups = rows // group
    slice_columns = 2 * half
    lanes = kept.shape[3]
    partner = at_img(y, other)
    steps = [(dx, dz) for dx in range(SIDE) for dz in range(SIDE) if (dx, dz) != (0, 0)]
    ori_peers = [at_ori(ring(x, dx), ring(z, dz)) for dx, dz in steps]
    img_peers = [partner] + [at_img(ring(y, d), cc) for d in range(1, SIDE) for cc in range(CORES)]
    neighbours = [at_ori(ring(x, 1), z), at_ori(ring(x, -1), z), at_ori(x, ring(z, 1)), at_ori(x, ring(z, -1))]


    def columns(m, part):
        return images.at[:, pl.ds(pl.multiple_of(m * slice_columns + part * half, LANES), half)]

    def line(part):
        return (xa, x) if part == 0 else (xb, z)

    home = []
    for part in range(2):
        ref, place = line(part)
        home.append(pltpu.make_async_copy(columns(me, part), ref.at[place, me], load_sem.at[part]))
    load = pltpu.make_async_copy(
        projections.at[:, pl.ds(pl.multiple_of(me * slice_columns, LANES), slice_columns)], proj, load_sem.at[2]
    )
    for copy in home + [load]:
        copy.start()
    told[me] = slot_table(search)
    greet(img_peers + ori_peers)
    receivers = [(0, other)] + [(d, cc) for d in (1 + 2 * c, 3 - 2 * c, 2) for cc in range(CORES)]
    tells, turns = [], {}
    for k, (d, cc) in enumerate(receivers):
        tells.append(remote(told.at[me], told.at[me], told_send.at[k], told_recv.at[d, c], at_img(ring(y, -d), cc)))
        tells[-1].start()

    def turn(ks):
        for k in ks:
            d, cc = receivers[k]
            for part in range(2):
                ref, place = line(part)
                turns[k, part] = remote(
                    columns(ring(y, -d) * CORES + cc, part),
                    ref.at[place, me],
                    turn_send.at[k, part],
                    turn_recv.at[d, c, part],
                    at_img(ring(y, -d), cc),
                )
                turns[k, part].start()

    turn(range(PLANES - 1))

    sources = [(0, c), (0, other), (1, 0), (3, 1), (3, 0), (1, 1), (2, 0), (2, 1)]

    def source(k):
        d, cc = sources[k]
        return ring(y, d) * CORES + cc

    near, far = {}, {}

    def start_near(k):
        d, cc = sources[k]
        for part in range(2):
            ref, place = line(part)
            block_ref = ref.at[place, source(k)]
            if k == 0:
                home[part].wait()
            else:
                remote(
                    block_ref, block_ref, turn_send.at[k - 1, part], turn_recv.at[d, cc, part], partner
                ).wait_recv()
            for way in (2 * part, 2 * part + 1):
                near[k, way] = remote(
                    block_ref, block_ref, near_send.at[k, way], near_recv.at[k, way], neighbours[way]
                )
                near[k, way].start()

    def start_far(k):
        for way in range(4):
            ref, place = line(way // 2)
            forward = way % 2 == 0
            near[k, way].wait_recv()
            block_ref = ref.at[ring(place, -1 if forward else 1), source(k), pl.ds(0 if forward else mid, mid)]
            far[k, way] = remote(block_ref, block_ref, far_send.at[k, way], far_recv.at[k, way], neighbours[way])
            far[k, way].start()

    def wait_far(k):
        for way in range(4):
            far[k, way].wait_recv()

    start_near(0)
    for d in range(SIDE):
        for cc in range(CORES) if d else (other,):
            tile = told.at[ring(y, d) * CORES + cc]
            remote(tile, tile, told_send.at[0], told_recv.at[d, cc], partner).wait_recv()
    sublane = lax.broadcasted_iota(jnp.int32, (PLANES, LANES), 0)
    gathered = told[0]
    for m in range(1, PLANES):
        gathered = jnp.where(sublane == m, told[m], gathered)
    tables[block] = gathered
    spreads = [
        remote(tables.at[block], tables.at[block], table_send.at[k], table_recv.at[k], peer)
        for k, peer in enumerate(ori_peers)
    ]
    for copy in spreads:
        copy.start()
    start_near(1)
    start_far(0)
    start_far(1)
    for copy in spreads:
        copy.wait_recv()
    lane_row = lax.broadcasted_iota(jnp.int32, (LANES, LANES), 0)
    homes = [
        jnp.concatenate([tables[p * SIDE + z] for p in range(SIDE)], axis=0),
        jnp.concatenate([tables[x * SIDE + p] for p in range(SIDE)], axis=0),
    ]
    for d in range(SIDE):
        for s in range(SLOTS):
            for part, dest in enumerate((x * SIDE + ring(z, d), ring(x, d) * SIDE + z)):
                column = jnp.where(lane_row == s * BLOCKS + dest, 1.0, 0.0)
                pick = jnp.dot(homes[part], column, preferred_element_type=jnp.float32)
                for p in range(SIDE):
                    picks[part, d, s, p] = pick[p * PLANES : (p + 1) * PLANES]


    order = ORDER

    def fill(n):
        q, r = order[n]
        slot = n % AHEAD
        ys = [ring(y, d) for d in ROUNDS[r]]

        def step(cc, carry):
            m = (ys[0] + (ys[1] - ys[0]) * cc) * CORES + cc
            for part, (ref, place) in enumerate(((xa, z), (xb, x))):
                p = ring(q, -place)
                choices = [ref[p, m, g * group : (g + 1) * group, :] for g in range(groups)]
                for d in range(SIDE):
                    for s in range(SLOTS):
                        pick = jnp.broadcast_to(picks[part, d, s, p, pl.ds(m, 1), :], (group, LANES))
                        pick = jnp.concatenate([pick.astype(jnp.bfloat16)] * (half // LANES), axis=1)
                        value = choices[0]
                        for g in range(1, groups):
                            value = jnp.where(pick == g, choices[g], value)
                        if d and part == 0:
                            out_a[slot, d - 1, cc, s] = value
                        elif d:
                            out_b[slot, d - 1, cc, s] = value
                        elif part == 0:
                            arrived[q, r, cc, s, z, :, 0:half] = value
                        else:
                            arrived[q, r, cc, s, p, :, half : 2 * half] = value
            return carry

        lax.fori_loop(0, CORES, step, 0)

    moves = {}

    def send(n):
        q, r = order[n]
        slot = n % AHEAD
        moves[n] = []
        for d in (2, 1, 3):
            moves[n].append(
                remote(
                    out_a.at[slot, d - 1],
                    arrived.at[q, r, :, :, z, :, pl.ds(0, half)],
                    a_send.at[slot, d - 1],
                    a_recv.at[n, d - 1],
                    at_ori(x, ring(z, d)),
                )
            )
            moves[n].append(
                remote(
                    out_b.at[slot, d - 1],
                    arrived.at[q, r, :, :, ring(q, -x), :, pl.ds(half, half)],
                    b_send.at[slot, d - 1],
                    b_recv.at[n, d - 1],
                    at_ori(ring(x, d), z),
                )
            )
        for copy in moves[n]:
            copy.start()

    wait_far(0)
    wait_far(1)
    fill(0)
    send(0)
    for k in range(2, 6):
        start_near(k)
    start_far(2)
    start_far(3)
    start_near(6)
    start_near(7)
    start_far(4)
    start_far(5)
    wait_far(2)
    wait_far(3)
    fill(1)
    send(1)
    start_far(6)
    start_far(7)
    wait_far(4)
    wait_far(5)
    fill(2)
    send(2)
    for copy in tells + list(turns.values()) + spreads:
        copy.wait_send()
    load.wait()
    wide = proj[...].astype(jnp.float32)
    half_norm = 0.5 * jnp.sum(wide * wide, axis=1, keepdims=True)


    pairs, sums, thirds = {}, {}, {}
    last = SIDE - 1
    mid_ori = kept.shape[2] // 2

    def refill(n):
        for copy in moves[n]:
            copy.wait_send()
        fill(n + AHEAD)
        send(n + AHEAD)

    def begin(n):
        q, r = order[n]
        slot = n % 2
        if n >= 2:
            pairs[n - 2].wait_send()
        values = arrived[q, r].reshape(CORES * lanes, slice_columns)
        value = lax.dot_general(proj[...], values, (((1,), (1,)), ((), ())), preferred_element_type=jnp.float32)
        value = value - half_norm
        for cc in range(CORES):
            pair_out[slot, cc] = value[:, cc * lanes : (cc + 1) * lanes]
        pairs[n] = remote(pair_out.at[slot, other], pair_in.at[n], pair_send.at[slot], pair_recv.at[n], partner)
        pairs[n].start()

    def finish(n):
        q, r = order[n]
        pairs[n].wait_recv()
        kept[q, r] = pair_out[n % 2, c] + pair_in[n]
        if r == 0 and q in RELAYED:
            for h, step in ((0, 1), (1, -1)):
                rows_h = pl.ds(h * mid_ori, mid_ori)
                thirds[q, h] = remote(
                    kept.at[q, r, rows_h], y_half.at[q, h], h_send.at[q, h], h_recv.at[q, h], at_img(ring(y, step), c)
                )
                thirds[q, h].start()
        elif r == 0:
            sums[n] = remote(kept.at[q, r], y_in.at[q, 2], y_send.at[q, 2], y_recv.at[q, 2], at_img(ring(y, 2), c))
            sums[n].start()
        elif r < last and q not in RELAYED:
            pass_on(n)

    def pass_on(n):
        q, r = order[n]
        d0, d1 = ROUNDS[r]
        d = d0 + (d1 - d0) * c
        h = lax.div(d, 2)
        if q in RELAYED:
            half_ref = y_half.at[q, h]
            remote(half_ref, half_ref, h_send.at[q, h], h_recv.at[q, h], partner).wait_recv()
            rows_h = pl.ds(pl.multiple_of(h * mid_ori, 8), mid_ori)
            kept[q, r, rows_h, :] = kept[q, r, rows_h, :] + y_half[q, h]
        sums[n] = remote(kept.at[q, r], y_in.at[q, h], y_send.at[q, h], y_recv.at[q, h], at_img(ring(y, d), c))
        sums[n].start()


    shares = {}

    def share(q):
        for n, copy in sums.items():
            if order[n][0] == q:
                copy.wait_recv()
        value = kept[q, last] + y_in[q, 0] + y_in[q, 1]
        if q not in RELAYED:
            value = value + y_in[q, 2]
        kept[q, last] = value
        highest = jnp.max(kept[q, last], axis=0, keepdims=True)
        value = jnp.exp(kept[q, last] - highest)
        resp[q, 0, c] = value.astype(jnp.bfloat16)
        mass = jnp.sum(value, axis=0, keepdims=True)
        which = lax.broadcasted_iota(jnp.int32, (8, lanes), 0)
        stats[q, block] = jnp.where(which == 0, highest, mass)
        shares[q] = [
            remote(stats.at[q, block], stats.at[q, block], stat_send.at[q, k], stat_recv.at[q, k], peer)
            for k, peer in enumerate(ori_peers)
        ]
        for copy in shares[q]:
            copy.start()

    images_batch = lanes // SLOTS
    home_row = lax.broadcasted_iota(jnp.int32, (BLOCKS, lanes), 0)
    home_lane = lax.broadcasted_iota(jnp.int32, (BLOCKS, lanes), 1)
    lane_z = lax.rem(lax.div(home_lane, group), SIDE)

    here = lax.rem(x + z, BATCHES)
    lane = lax.broadcasted_iota(jnp.int32, (1, lanes), 1)
    factors = {}

    def fold(value, operation):
        return operation(value, pltpu.roll(value, images_batch, 1))

    def respond(q):
        spot = lax.rem(q - lane_z + SIDE, SIDE) * SIDE + lane_z
        widen = jnp.where(home_row == spot, 1.0, 0.0)
        plane = tables[:, pl.ds(me, 1), :].reshape(BLOCKS, LANES)
        named = lax.dot_general(plane, widen, (((0,), (0,)), ((), ())), preferred_element_type=jnp.float32)
        named = jnp.where(home_lane < images_batch, named[:BLOCKS], named[BLOCKS : 2 * BLOCKS])
        own = jnp.sum(jnp.where(home_row == block, named, 0.0), axis=0, keepdims=True)
        for copy in shares[q]:
            copy.wait()
        tops, masses = stats[q, :, 0, :], stats[q, :, 1, :]
        norm = jnp.zeros((1, lanes), jnp.float32)
        row = jnp.zeros((1, lanes), jnp.float32) if q == 0 else result[...]
        for g in range(groups):
            listed = named == g
            top = fold(jnp.max(jnp.where(listed, tops, NO_SCORE), axis=0, keepdims=True), jnp.maximum)
            mass = jnp.where(listed, jnp.exp(jnp.minimum(tops - top, 0.0)) * masses, 0.0)
            mass = fold(jnp.sum(mass, axis=0, keepdims=True), jnp.add)
            value = top + jnp.log(mass)
            moved = pltpu.roll(value, lax.rem((g - z) * group + lanes, lanes), 1)
            row = jnp.where((lax.div(lane, group) == g) & (here == q), moved, row)
            norm = jnp.where(own == g, value, norm)
        result[...] = row
        value = jnp.where(own >= 0, jnp.exp(stats[q, pl.ds(block, 1), 0, :] - norm), 0.0)
        scale[q, 0, c] = jnp.broadcast_to(value, (8, lanes))
        factors[q] = []
        for k, (d, cc) in enumerate(receivers):
            factors[q].append(
                remote(
                    scale.at[q, 0, c], scale.at[q, d, c], f_send.at[q, k], f_recv.at[q, d, c], at_img(ring(y, -d), cc)
                )
            )
            factors[q][-1].start()


    direct, passed, crossed = {}, {}, {}

    def cross(q, d):
        crossed[q, d] = remote(resp.at[q, d, c], resp.at[q, d, c], rc_send.at[q, d], rc_recv.at[q, d], partner)
        crossed[q, d].start()

    def part_of(q, d, h):
        return resp.at[q, d, c, pl.ds(h * mid_ori, mid_ori)]

    def gather_near(q):
        cross(q, 0)
        for step in range(2):
            for d, h in ((1, step), (3, 1 - step)):
                direct[q, d, h] = remote(
                    part_of(q, 0, h), part_of(q, d, h), r_send.at[q, d, h], r_recv.at[q, d, h], at_img(ring(y, -d), c)
                )
                direct[q, d, h].start()

    def gather_direct(q):
        cross(q, 0)
        for d in (2, 1, 3):
            direct[q, d] = remote(
                resp.at[q, 0, c], resp.at[q, d, c], r_send.at[q, d, 0], r_recv.at[q, d, 0], at_img(ring(y, -d), c)
            )
            direct[q, d].start()

    def gather_far(q):
        for d, h in ((1, 0), (3, 1)):
            direct[q, d, h].wait_recv()
            passed[q, h] = remote(
                part_of(q, d, h), part_of(q, 2, h), r_send.at[q, 2, h], r_recv.at[q, 2, h], at_img(ring(y, -d), c)
            )
            passed[q, h].start()
        for d, h in ((1, 1), (3, 0)):
            direct[q, d, h].wait_recv()
            cross(q, d)

    def gather_last(q):
        for h in range(2):
            passed[q, h].wait_recv()
        cross(q, 2)

    tile = 2 * LANES

    def add(parts, first=False, final=False):
        for q, d in parts:
            crossed[q, d].wait_recv()
            for cc in range(CORES) if d else (other,):
                ref = scale.at[q, d, cc]
                remote(ref, ref, f_send.at[q, 0], f_recv.at[q, d, cc], partner).wait_recv()
        pieces = [(q, d, cc) for q, d in parts for cc in range(CORES)]
        factor = jnp.concatenate(
            [(resp[q, d, cc].astype(jnp.float32) * scale[q, d, cc, 0:1, :]).astype(jnp.bfloat16) for q, d, cc in pieces],
            axis=1,
        )
        for t in range(slice_columns // tile):
            cols = slice(t * tile, (t + 1) * tile)
            values = []
            for q, d, cc in pieces:
                r = [pair[cc] for pair in ROUNDS].index(d)
                values.append(arrived[q, r, cc, :, :, :, cols].reshape(lanes, tile))
            part = jnp.dot(factor, jnp.concatenate(values, axis=0), preferred_element_type=jnp.float32)
            if not first:
                part = part + total[:, cols]
            if final:
                weighted[:, cols] = part.astype(weighted.dtype)
            else:
                total[:, cols] = part

    passes_at = {7: (6,), 8: (7,), 10: (9,), 11: (10,), 12: (12,), 13: (13,)}
    for n in range(len(order)):
        for copy in moves[n]:
            copy.wait_recv()
        if n == 8:
            share(0)
            gather_near(0)
        if n == 1:
            wait_far(6)
            wait_far(7)
        if n + AHEAD < len(order):
            refill(n)
        begin(n)
        if 0 < n <= 11:
            finish(n - 1)
        if n >= 11:
            finish(n)
        for k in passes_at.get(n, ()):
            pass_on(k)
        if n == 9:
            gather_far(0)
        if n == 10:
            respond(0)
            share(1)
            gather_near(1)
        if n == 11:
            gather_last(0)
        if n == 13:
            gather_far(1)
            respond(1)
            add([(0, d) for d in range(SIDE)], first=True)
        if n == 14:
            share(2)
            gather_near(2)
    share(3)
    gather_direct(3)
    gather_last(1)
    add([(1, d) for d in range(SIDE)])
    respond(2)
    gather_far(2)
    respond(3)
    add([(2, 0), (2, 1), (2, 3), (3, 0)])
    for d in (2, 1, 3):
        direct[3, d].wait_recv()
        cross(3, d)
    gather_last(2)
    add([(3, 2), (3, 1), (3, 3), (2, 2)], final=True)
    loglik[...] = result[:, 0 : loglik.shape[1]]

    for copy in list(near.values()) + list(far.values()):
        copy.wait_send()
    for n in range(len(order) - AHEAD, len(order)):
        for copy in moves[n]:
            copy.wait_send()
    for n in (len(order) - 2, len(order) - 1):
        pairs[n].wait_send()
    for q in range(BATCHES):
        for copy in factors[q]:
            copy.wait_send()
    for copies in (sums, thirds, direct, passed, crossed):
        for copy in copies.values():
            copy.wait_send()


def per_device(images, projections, search):
    groups, _ = search.shape
    rows, columns = images.shape
    group = rows // groups
    slice_columns = columns // PLANES
    half = slice_columns // 2
    oris = projections.shape[0]
    lanes = BLOCKS * SLOTS * group // BATCHES
    peers, rounds = SIDE - 1, BATCHES * SIDE
    mid_ori = oris // 2

    vmem, anywhere = pl.BlockSpec(memory_space=pltpu.VMEM), pl.BlockSpec(memory_space=pl.ANY)
    bf16, f32, dma = jnp.bfloat16, jnp.float32, pltpu.SemaphoreType.DMA
    weighted, loglik = pl.pallas_call(
        kernel,
        out_shape=(
            jax.ShapeDtypeStruct((oris, slice_columns), bf16),
            jax.ShapeDtypeStruct((1, rows), f32),
        ),
        in_specs=[pl.BlockSpec(memory_space=pltpu.SMEM), anywhere, anywhere],
        out_specs=(vmem, vmem),
        scratch_shapes=[
            pltpu.VMEM((SIDE, PLANES, rows, half), bf16),
            pltpu.VMEM((SIDE, PLANES, rows, half), bf16),
            pltpu.VMEM((PLANES, 8, LANES), f32),
            pltpu.VMEM((BLOCKS, PLANES, LANES), f32),
            pltpu.VMEM((2, SIDE, SLOTS, SIDE, PLANES, LANES), f32),
            pltpu.VMEM((oris, slice_columns), bf16),
            pltpu.VMEM((BATCHES, SIDE, CORES, SLOTS, SIDE, group, slice_columns), bf16),
            pltpu.VMEM((AHEAD, peers, CORES, SLOTS, group, half), bf16),
            pltpu.VMEM((AHEAD, peers, CORES, SLOTS, group, half), bf16),
            pltpu.VMEM((2, CORES, oris, lanes), f32),
            pltpu.VMEM((rounds, oris, lanes), f32),
            pltpu.VMEM((BATCHES, SIDE, oris, lanes), f32),
            pltpu.VMEM((BATCHES, 2, mid_ori, lanes), f32),
            pltpu.VMEM((BATCHES, peers, oris, lanes), f32),
            pltpu.VMEM((BATCHES, BLOCKS, 8, lanes), f32),
            pltpu.VMEM((BATCHES, SIDE, CORES, oris, lanes), bf16),
            pltpu.VMEM((BATCHES, SIDE, CORES, 8, lanes), f32),
            pltpu.VMEM((1, lanes), f32),
            pltpu.VMEM((oris, slice_columns), f32),
            dma((3,)),
            dma((PLANES - 1, 2)),
            dma((SIDE, CORES, 2)),
            dma((PLANES - 1,)),
            dma((SIDE, CORES)),
            dma((BLOCKS - 1,)),
            dma((BLOCKS - 1,)),
            dma((PLANES, 4)),
            dma((PLANES, 4)),
            dma((PLANES, 4)),
            dma((PLANES, 4)),
            dma((AHEAD, peers)),
            dma((rounds, peers)),
            dma((AHEAD, peers)),
            dma((rounds, peers)),
            dma((2,)),
            dma((rounds,)),
            dma((BATCHES, 2)),
            dma((BATCHES, 2)),
            dma((BATCHES, peers)),
            dma((BATCHES, peers)),
            dma((BATCHES, BLOCKS - 1)),
            dma((BATCHES, BLOCKS - 1)),
            dma((BATCHES, SIDE, 2)),
            dma((BATCHES, SIDE, 2)),
            dma((BATCHES, SIDE)),
            dma((BATCHES, SIDE)),
            dma((BATCHES, PLANES - 1)),
            dma((BATCHES, SIDE, CORES)),
        ],
        compiler_params=pltpu.CompilerParams(collective_id=0, has_side_effects=True, vmem_limit_bytes=62 * 2**20),
        cost_estimate=pl.CostEstimate(flops=15 * 10**9, bytes_accessed=32 * 2**20, transcendentals=10**6),
    )(search, images, projections)
    return weighted, loglik.reshape(-1)


def solution(mesh):
    placed = (P(("img", "ori"), None), P("ori", None), P(("img", "ori"), None))
    return jax.shard_map(
        per_device,
        mesh=mesh,
        in_specs=placed,
        out_specs=(P("ori", "img"), P(("img", "ori"))),
        check_vma=False,
    )
```

```python
import jax
import jax.numpy as jnp
from jax import lax
from jax.experimental import pallas as pl
from jax.experimental.pallas import tpu as pltpu
from jax.sharding import PartitionSpec as P

MESH = pl.DeviceIdType.MESH
SIDE = 4
CORES = 2
PLANES = SIDE * CORES
BLOCKS = SIDE * SIDE
SLOTS = 2
LANES = 128
BATCHES = SIDE
AHEAD = 3
NO_SCORE = -3.0e38

ROUNDS = [(2, 2), (1, 3), (3, 1), (0, 0)]
ORDER = [(0, 3), (0, 1), (0, 2), (1, 3), (0, 0), (1, 0), (1, 1), (1, 2)]
ORDER += [(2, 0), (2, 1), (2, 2), (3, 0), (3, 1), (3, 2), (2, 3), (3, 3)]
RELAYED = (1, 2, 3)


def ring(position, step):
    return lax.rem(position + step + SIDE, SIDE)


def at_img(y, c):
    return {"img": y * CORES + c, "ori": lax.axis_index("ori")}


def at_ori(x, z):
    return {"img": lax.axis_index("img"), "ori": x * SIDE + z}


def remote(source, target, send, recv, device):
    return pltpu.make_async_remote_copy(
        src_ref=source,
        dst_ref=target,
        send_sem=send,
        recv_sem=recv,
        device_id=device,
        device_id_type=MESH,
    )


def greet(devices):
    barrier = pltpu.get_barrier_semaphore()
    for device in devices:
        pl.semaphore_signal(barrier, inc=1, device_id=device, device_id_type=MESH)
    pl.semaphore_wait(barrier, len(devices))


def slot_table(search):
    lane = lax.broadcasted_iota(jnp.int32, (8, LANES), 1)
    b, s = lax.rem(lane, BLOCKS), lax.div(lane, BLOCKS)
    table = jnp.full((8, LANES), -1.0, jnp.float32)
    rank = jnp.zeros((8, LANES), jnp.int32)
    for g in range(search.shape[0]):
        hit = b == search[g, 0]
        for n in range(1, search.shape[1]):
            hit = hit | (b == search[g, n])
        table = jnp.where(hit & (rank == s), float(g), table)
        rank = rank + hit.astype(jnp.int32)
    return table


def kernel(
    search,
    images,
    projections,
    weighted,
    loglik,
    xa,
    xb,
    told,
    tables,
    picks,
    proj,
    arrived,
    out_a,
    out_b,
    pair_out,
    pair_in,
    kept,
    y_half,
    y_in,
    stats,
    resp,
    scale,
    result,
    total,
    load_sem,
    turn_send,
    turn_recv,
    told_send,
    told_recv,
    table_send,
    table_recv,
    near_send,
    near_recv,
    far_send,
    far_recv,
    a_send,
    a_recv,
    b_send,
    b_recv,
    pair_send,
    pair_recv,
    h_send,
    h_recv,
    y_send,
    y_recv,
    stat_send,
    stat_recv,
    r_send,
    r_recv,
    rc_send,
    rc_recv,
    f_send,
    f_recv,
):
    me, block = lax.axis_index("img"), lax.axis_index("ori")
    y, c = lax.div(me, CORES), lax.rem(me, CORES)
    x, z = lax.div(block, SIDE), lax.rem(block, SIDE)
    other = 1 - c
    rows, half = xa.shape[2], xa.shape[3]
    mid = rows // 2
    group = arrived.shape[5]
    groups = rows // group
    slice_columns = 2 * half
    lanes = kept.shape[3]
    partner = at_img(y, other)
    steps = [(dx, dz) for dx in range(SIDE) for dz in range(SIDE) if (dx, dz) != (0, 0)]
    ori_peers = [at_ori(ring(x, dx), ring(z, dz)) for dx, dz in steps]
    img_peers = [partner] + [at_img(ring(y, d), cc) for d in range(1, SIDE) for cc in range(CORES)]
    neighbours = [at_ori(ring(x, 1), z), at_ori(ring(x, -1), z), at_ori(x, ring(z, 1)), at_ori(x, ring(z, -1))]


    def columns(m, part):
        return images.at[:, pl.ds(pl.multiple_of(m * slice_columns + part * half, LANES), half)]

    def line(part):
        return (xa, x) if part == 0 else (xb, z)

    home = []
    for part in range(2):
        ref, place = line(part)
        home.append(pltpu.make_async_copy(columns(me, part), ref.at[place, me], load_sem.at[part]))
    load = pltpu.make_async_copy(
        projections.at[:, pl.ds(pl.multiple_of(me * slice_columns, LANES), slice_columns)], proj, load_sem.at[2]
    )
    for copy in home + [load]:
        copy.start()
    told[me] = slot_table(search)
    greet(img_peers + ori_peers)
    receivers = [(0, other)] + [(d, cc) for d in (1 + 2 * c, 3 - 2 * c, 2) for cc in range(CORES)]
    tells, turns = [], {}
    for k, (d, cc) in enumerate(receivers):
        tells.append(remote(told.at[me], told.at[me], told_send.at[k], told_recv.at[d, c], at_img(ring(y, -d), cc)))
        tells[-1].start()

    def turn(ks):
        for k in ks:
            d, cc = receivers[k]
            for part in range(2):
                ref, place = line(part)
                turns[k, part] = remote(
                    columns(ring(y, -d) * CORES + cc, part),
                    ref.at[place, me],
                    turn_send.at[k, part],
                    turn_recv.at[d, c, part],
                    at_img(ring(y, -d), cc),
                )
                turns[k, part].start()

    turn(range(PLANES - 1))

    sources = [(0, c), (0, other), (1, 0), (3, 1), (3, 0), (1, 1), (2, 0), (2, 1)]

    def source(k):
        d, cc = sources[k]
        return ring(y, d) * CORES + cc

    near, far = {}, {}

    def start_near(k):
        d, cc = sources[k]
        for part in range(2):
            ref, place = line(part)
            block_ref = ref.at[place, source(k)]
            if k == 0:
                home[part].wait()
            else:
                remote(
                    block_ref, block_ref, turn_send.at[k - 1, part], turn_recv.at[d, cc, part], partner
                ).wait_recv()
            for way in (2 * part, 2 * part + 1):
                near[k, way] = remote(
                    block_ref, block_ref, near_send.at[k, way], near_recv.at[k, way], neighbours[way]
                )
                near[k, way].start()

    def start_far(k):
        for way in range(4):
            ref, place = line(way // 2)
            forward = way % 2 == 0
            near[k, way].wait_recv()
            block_ref = ref.at[ring(place, -1 if forward else 1), source(k), pl.ds(0 if forward else mid, mid)]
            far[k, way] = remote(block_ref, block_ref, far_send.at[k, way], far_recv.at[k, way], neighbours[way])
            far[k, way].start()

    def wait_far(k):
        for way in range(4):
            far[k, way].wait_recv()

    start_near(0)
    for d in range(SIDE):
        for cc in range(CORES) if d else (other,):
            tile = told.at[ring(y, d) * CORES + cc]
            remote(tile, tile, told_send.at[0], told_recv.at[d, cc], partner).wait_recv()
    sublane = lax.broadcasted_iota(jnp.int32, (PLANES, LANES), 0)
    gathered = told[0]
    for m in range(1, PLANES):
        gathered = jnp.where(sublane == m, told[m], gathered)
    tables[block] = gathered
    spreads = [
        remote(tables.at[block], tables.at[block], table_send.at[k], table_recv.at[k], peer)
        for k, peer in enumerate(ori_peers)
    ]
    for copy in spreads:
        copy.start()
    start_near(1)
    start_far(0)
    start_far(1)
    for copy in spreads:
        copy.wait_recv()
    lane_row = lax.broadcasted_iota(jnp.int32, (LANES, LANES), 0)
    homes = [
        jnp.concatenate([tables[p * SIDE + z] for p in range(SIDE)], axis=0),
        jnp.concatenate([tables[x * SIDE + p] for p in range(SIDE)], axis=0),
    ]
    for d in range(SIDE):
        for s in range(SLOTS):
            for part, dest in enumerate((x * SIDE + ring(z, d), ring(x, d) * SIDE + z)):
                column = jnp.where(lane_row == s * BLOCKS + dest, 1.0, 0.0)
                pick = jnp.dot(homes[part], column, preferred_element_type=jnp.float32)
                for p in range(SIDE):
                    picks[part, d, s, p] = pick[p * PLANES : (p + 1) * PLANES]


    order = ORDER

    def fill(n):
        q, r = order[n]
        slot = n % AHEAD
        ys = [ring(y, d) for d in ROUNDS[r]]

        def step(cc, carry):
            m = (ys[0] + (ys[1] - ys[0]) * cc) * CORES + cc
            for part, (ref, place) in enumerate(((xa, z), (xb, x))):
                p = ring(q, -place)
                choices = [ref[p, m, g * group : (g + 1) * group, :] for g in range(groups)]
                for d in range(SIDE):
                    for s in range(SLOTS):
                        pick = jnp.broadcast_to(picks[part, d, s, p, pl.ds(m, 1), :], (group, LANES))
                        pick = jnp.concatenate([pick.astype(jnp.bfloat16)] * (half // LANES), axis=1)
                        value = choices[0]
                        for g in range(1, groups):
                            value = jnp.where(pick == g, choices[g], value)
                        if d and part == 0:
                            out_a[slot, d - 1, cc, s] = value
                        elif d:
                            out_b[slot, d - 1, cc, s] = value
                        elif part == 0:
                            arrived[q, r, cc, s, z, :, 0:half] = value
                        else:
                            arrived[q, r, cc, s, p, :, half : 2 * half] = value
            return carry

        lax.fori_loop(0, CORES, step, 0)

    moves = {}

    def send(n):
        q, r = order[n]
        slot = n % AHEAD
        moves[n] = []
        for d in (2, 1, 3):
            moves[n].append(
                remote(
                    out_a.at[slot, d - 1],
                    arrived.at[q, r, :, :, z, :, pl.ds(0, half)],
                    a_send.at[slot, d - 1],
                    a_recv.at[n, d - 1],
                    at_ori(x, ring(z, d)),
                )
            )
            moves[n].append(
                remote(
                    out_b.at[slot, d - 1],
                    arrived.at[q, r, :, :, ring(q, -x), :, pl.ds(half, half)],
                    b_send.at[slot, d - 1],
                    b_recv.at[n, d - 1],
                    at_ori(ring(x, d), z),
                )
            )
        for copy in moves[n]:
            copy.start()

    wait_far(0)
    wait_far(1)
    fill(0)
    send(0)
    for k in range(2, 6):
        start_near(k)
    start_far(2)
    start_far(3)
    start_near(6)
    start_near(7)
    start_far(4)
    start_far(5)
    wait_far(2)
    wait_far(3)
    fill(1)
    send(1)
    start_far(6)
    start_far(7)
    wait_far(4)
    wait_far(5)
    fill(2)
    send(2)
    for copy in tells + list(turns.values()) + spreads:
        copy.wait_send()
    load.wait()
    wide = proj[...].astype(jnp.float32)
    half_norm = 0.5 * jnp.sum(wide * wide, axis=1, keepdims=True)


    pairs, sums, thirds = {}, {}, {}
    last = SIDE - 1
    mid_ori = kept.shape[2] // 2

    def refill(n):
        for copy in moves[n]:
            copy.wait_send()
        fill(n + AHEAD)
        send(n + AHEAD)

    def begin(n):
        q, r = order[n]
        slot = n % 2
        if n >= 2:
            pairs[n - 2].wait_send()
        values = arrived[q, r].reshape(CORES * lanes, slice_columns)
        value = lax.dot_general(proj[...], values, (((1,), (1,)), ((), ())), preferred_element_type=jnp.float32)
        value = value - half_norm
        for cc in range(CORES):
            pair_out[slot, cc] = value[:, cc * lanes : (cc + 1) * lanes]
        pairs[n] = remote(pair_out.at[slot, other], pair_in.at[n], pair_send.at[slot], pair_recv.at[n], partner)
        pairs[n].start()

    def finish(n):
        q, r = order[n]
        pairs[n].wait_recv()
        kept[q, r] = pair_out[n % 2, c] + pair_in[n]
        if r == 0 and q in RELAYED:
            for h, step in ((0, 1), (1, -1)):
                rows_h = pl.ds(h * mid_ori, mid_ori)
                thirds[q, h] = remote(
                    kept.at[q, r, rows_h], y_half.at[q, h], h_send.at[q, h], h_recv.at[q, h], at_img(ring(y, step), c)
                )
                thirds[q, h].start()
        elif r == 0:
            sums[n] = remote(kept.at[q, r], y_in.at[q, 2], y_send.at[q, 2], y_recv.at[q, 2], at_img(ring(y, 2), c))
            sums[n].start()
        elif r < last and q not in RELAYED:
            pass_on(n)

    def pass_on(n):
        q, r = order[n]
        d0, d1 = ROUNDS[r]
        d = d0 + (d1 - d0) * c
        h = lax.div(d, 2)
        if q in RELAYED:
            half_ref = y_half.at[q, h]
            remote(half_ref, half_ref, h_send.at[q, h], h_recv.at[q, h], partner).wait_recv()
            rows_h = pl.ds(pl.multiple_of(h * mid_ori, 8), mid_ori)
            kept[q, r, rows_h, :] = kept[q, r, rows_h, :] + y_half[q, h]
        sums[n] = remote(kept.at[q, r], y_in.at[q, h], y_send.at[q, h], y_recv.at[q, h], at_img(ring(y, d), c))
        sums[n].start()


    shares = {}

    def share(q):
        for n, copy in sums.items():
            if order[n][0] == q:
                copy.wait_recv()
        value = kept[q, last] + y_in[q, 0] + y_in[q, 1]
        if q not in RELAYED:
            value = value + y_in[q, 2]
        kept[q, last] = value
        highest = jnp.max(kept[q, last], axis=0, keepdims=True)
        value = jnp.exp(kept[q, last] - highest)
        resp[q, 0, c] = value.astype(jnp.bfloat16)
        mass = jnp.sum(value, axis=0, keepdims=True)
        which = lax.broadcasted_iota(jnp.int32, (8, lanes), 0)
        stats[q, block] = jnp.where(which == 0, highest, mass)
        shares[q] = [
            remote(stats.at[q, block], stats.at[q, block], stat_send.at[q, k], stat_recv.at[q, k], peer)
            for k, peer in enumerate(ori_peers)
        ]
        for copy in shares[q]:
            copy.start()

    images_batch = lanes // SLOTS
    home_row = lax.broadcasted_iota(jnp.int32, (BLOCKS, lanes), 0)
    home_lane = lax.broadcasted_iota(jnp.int32, (BLOCKS, lanes), 1)
    lane_z = lax.rem(lax.div(home_lane, group), SIDE)

    here = lax.rem(x + z, BATCHES)
    lane = lax.broadcasted_iota(jnp.int32, (1, lanes), 1)
    factors = {}

    def fold(value, operation):
        return operation(value, pltpu.roll(value, images_batch, 1))

    def respond(q):
        spot = lax.rem(q - lane_z + SIDE, SIDE) * SIDE + lane_z
        widen = jnp.where(home_row == spot, 1.0, 0.0)
        plane = tables[:, pl.ds(me, 1), :].reshape(BLOCKS, LANES)
        named = lax.dot_general(plane, widen, (((0,), (0,)), ((), ())), preferred_element_type=jnp.float32)
        named = jnp.where(home_lane < images_batch, named[:BLOCKS], named[BLOCKS : 2 * BLOCKS])
        own = jnp.sum(jnp.where(home_row == block, named, 0.0), axis=0, keepdims=True)
        for copy in shares[q]:
            copy.wait()
        tops, masses = stats[q, :, 0, :], stats[q, :, 1, :]
        norm = jnp.zeros((1, lanes), jnp.float32)
        row = jnp.zeros((1, lanes), jnp.float32) if q == 0 else result[...]
        for g in range(groups):
            listed = named == g
            top = fold(jnp.max(jnp.where(listed, tops, NO_SCORE), axis=0, keepdims=True), jnp.maximum)
            mass = jnp.where(listed, jnp.exp(jnp.minimum(tops - top, 0.0)) * masses, 0.0)
            mass = fold(jnp.sum(mass, axis=0, keepdims=True), jnp.add)
            value = top + jnp.log(mass)
            moved = pltpu.roll(value, lax.rem((g - z) * group + lanes, lanes), 1)
            row = jnp.where((lax.div(lane, group) == g) & (here == q), moved, row)
            norm = jnp.where(own == g, value, norm)
        result[...] = row
        value = jnp.where(own >= 0, jnp.exp(stats[q, pl.ds(block, 1), 0, :] - norm), 0.0)
        scale[q, 0, c] = jnp.broadcast_to(value, (8, lanes))
        factors[q] = []
        for k, (d, cc) in enumerate(receivers):
            factors[q].append(
                remote(
                    scale.at[q, 0, c], scale.at[q, d, c], f_send.at[q, k], f_recv.at[q, d, c], at_img(ring(y, -d), cc)
                )
            )
            factors[q][-1].start()


    direct, passed, crossed = {}, {}, {}

    def cross(q, d):
        crossed[q, d] = remote(resp.at[q, d, c], resp.at[q, d, c], rc_send.at[q, d], rc_recv.at[q, d], partner)
        crossed[q, d].start()

    def part_of(q, d, h):
        return resp.at[q, d, c, pl.ds(h * mid_ori, mid_ori)]

    def gather_near(q):
        cross(q, 0)
        for step in range(2):
            for d, h in ((1, step), (3, 1 - step)):
                direct[q, d, h] = remote(
                    part_of(q, 0, h), part_of(q, d, h), r_send.at[q, d, h], r_recv.at[q, d, h], at_img(ring(y, -d), c)
                )
                direct[q, d, h].start()

    def gather_far(q):
        for d, h in ((1, 0), (3, 1)):
            direct[q, d, h].wait_recv()
            passed[q, h] = remote(
                part_of(q, d, h), part_of(q, 2, h), r_send.at[q, 2, h], r_recv.at[q, 2, h], at_img(ring(y, -d), c)
            )
            passed[q, h].start()
        for d, h in ((1, 1), (3, 0)):
            direct[q, d, h].wait_recv()
            cross(q, d)

    def gather_last(q):
        for h in range(2):
            passed[q, h].wait_recv()
        cross(q, 2)

    tile = 2 * LANES

    def add(parts, first=False, final=False):
        for q, d in parts:
            crossed[q, d].wait_recv()
            for cc in range(CORES) if d else (other,):
                ref = scale.at[q, d, cc]
                remote(ref, ref, f_send.at[q, 0], f_recv.at[q, d, cc], partner).wait_recv()
        pieces = [(q, d, cc) for q, d in parts for cc in range(CORES)]
        factor = jnp.concatenate(
            [(resp[q, d, cc].astype(jnp.float32) * scale[q, d, cc, 0:1, :]).astype(jnp.bfloat16) for q, d, cc in pieces],
            axis=1,
        )
        for t in range(slice_columns // tile):
            cols = slice(t * tile, (t + 1) * tile)
            values = []
            for q, d, cc in pieces:
                r = [pair[cc] for pair in ROUNDS].index(d)
                values.append(arrived[q, r, cc, :, :, :, cols].reshape(lanes, tile))
            part = jnp.dot(factor, jnp.concatenate(values, axis=0), preferred_element_type=jnp.float32)
            if not first:
                part = part + total[:, cols]
            if final:
                weighted[:, cols] = part.astype(weighted.dtype)
            else:
                total[:, cols] = part

    passes_at = {7: (6,), 8: (7,), 10: (9,), 11: (10,), 12: (12,), 13: (13,)}
    for n in range(len(order)):
        for copy in moves[n]:
            copy.wait_recv()
        if n == 8:
            share(0)
            gather_near(0)
        if n == 1:
            wait_far(6)
            wait_far(7)
        if n + AHEAD < len(order):
            refill(n)
        begin(n)
        if 0 < n <= 11:
            finish(n - 1)
        if n >= 11:
            finish(n)
        for k in passes_at.get(n, ()):
            pass_on(k)
        if n == 9:
            gather_far(0)
        if n == 10:
            respond(0)
            share(1)
            gather_near(1)
        if n == 11:
            gather_last(0)
        if n == 13:
            gather_far(1)
            respond(1)
            add([(0, d) for d in range(SIDE)], first=True)
        if n == 14:
            share(2)
            gather_near(2)
    share(3)
    gather_near(3)
    gather_last(1)
    add([(1, d) for d in range(SIDE)])
    respond(2)
    gather_far(2)
    respond(3)
    gather_far(3)
    add([(2, 0), (2, 1), (2, 3), (3, 0)])
    gather_last(2)
    gather_last(3)
    add([(3, 2), (3, 1), (3, 3), (2, 2)], final=True)
    loglik[...] = result[:, 0 : loglik.shape[1]]

    for copy in list(near.values()) + list(far.values()):
        copy.wait_send()
    for n in range(len(order) - AHEAD, len(order)):
        for copy in moves[n]:
            copy.wait_send()
    for n in (len(order) - 2, len(order) - 1):
        pairs[n].wait_send()
    for q in range(BATCHES):
        for copy in factors[q]:
            copy.wait_send()
    for copies in (sums, thirds, direct, passed, crossed):
        for copy in copies.values():
            copy.wait_send()


def per_device(images, projections, search):
    groups, _ = search.shape
    rows, columns = images.shape
    group = rows // groups
    slice_columns = columns // PLANES
    half = slice_columns // 2
    oris = projections.shape[0]
    lanes = BLOCKS * SLOTS * group // BATCHES
    peers, rounds = SIDE - 1, BATCHES * SIDE
    mid_ori = oris // 2

    vmem, anywhere = pl.BlockSpec(memory_space=pltpu.VMEM), pl.BlockSpec(memory_space=pl.ANY)
    bf16, f32, dma = jnp.bfloat16, jnp.float32, pltpu.SemaphoreType.DMA
    weighted, loglik = pl.pallas_call(
        kernel,
        out_shape=(
            jax.ShapeDtypeStruct((oris, slice_columns), bf16),
            jax.ShapeDtypeStruct((1, rows), f32),
        ),
        in_specs=[pl.BlockSpec(memory_space=pltpu.SMEM), anywhere, anywhere],
        out_specs=(vmem, vmem),
        scratch_shapes=[
            pltpu.VMEM((SIDE, PLANES, rows, half), bf16),
            pltpu.VMEM((SIDE, PLANES, rows, half), bf16),
            pltpu.VMEM((PLANES, 8, LANES), f32),
            pltpu.VMEM((BLOCKS, PLANES, LANES), f32),
            pltpu.VMEM((2, SIDE, SLOTS, SIDE, PLANES, LANES), f32),
            pltpu.VMEM((oris, slice_columns), bf16),
            pltpu.VMEM((BATCHES, SIDE, CORES, SLOTS, SIDE, group, slice_columns), bf16),
            pltpu.VMEM((AHEAD, peers, CORES, SLOTS, group, half), bf16),
            pltpu.VMEM((AHEAD, peers, CORES, SLOTS, group, half), bf16),
            pltpu.VMEM((2, CORES, oris, lanes), f32),
            pltpu.VMEM((rounds, oris, lanes), f32),
            pltpu.VMEM((BATCHES, SIDE, oris, lanes), f32),
            pltpu.VMEM((BATCHES, 2, mid_ori, lanes), f32),
            pltpu.VMEM((BATCHES, peers, oris, lanes), f32),
            pltpu.VMEM((BATCHES, BLOCKS, 8, lanes), f32),
            pltpu.VMEM((BATCHES, SIDE, CORES, oris, lanes), bf16),
            pltpu.VMEM((BATCHES, SIDE, CORES, 8, lanes), f32),
            pltpu.VMEM((1, lanes), f32),
            pltpu.VMEM((oris, slice_columns), f32),
            dma((3,)),
            dma((PLANES - 1, 2)),
            dma((SIDE, CORES, 2)),
            dma((PLANES - 1,)),
            dma((SIDE, CORES)),
            dma((BLOCKS - 1,)),
            dma((BLOCKS - 1,)),
            dma((PLANES, 4)),
            dma((PLANES, 4)),
            dma((PLANES, 4)),
            dma((PLANES, 4)),
            dma((AHEAD, peers)),
            dma((rounds, peers)),
            dma((AHEAD, peers)),
            dma((rounds, peers)),
            dma((2,)),
            dma((rounds,)),
            dma((BATCHES, 2)),
            dma((BATCHES, 2)),
            dma((BATCHES, peers)),
            dma((BATCHES, peers)),
            dma((BATCHES, BLOCKS - 1)),
            dma((BATCHES, BLOCKS - 1)),
            dma((BATCHES, SIDE, 2)),
            dma((BATCHES, SIDE, 2)),
            dma((BATCHES, SIDE)),
            dma((BATCHES, SIDE)),
            dma((BATCHES, PLANES - 1)),
            dma((BATCHES, SIDE, CORES)),
        ],
        compiler_params=pltpu.CompilerParams(collective_id=0, has_side_effects=True, vmem_limit_bytes=62 * 2**20),
        cost_estimate=pl.CostEstimate(flops=15 * 10**9, bytes_accessed=32 * 2**20, transcendentals=10**6),
    )(search, images, projections)
    return weighted, loglik.reshape(-1)


def solution(mesh):
    placed = (P(("img", "ori"), None), P("ori", None), P(("img", "ori"), None))
    return jax.shard_map(
        per_device,
        mesh=mesh,
        in_specs=placed,
        out_specs=(P("ori", "img"), P(("img", "ori"))),
        check_vma=False,
    )
```
